32 devices in a mesh: dp: 4 (over x, core), ctx: 8 (over z, y).
Axes of the slice: x: 2, y: 2, z: 4, core: 2. Of those that a mesh axis runs over, the one named last changes fastest.
Arguments:
- feats: bfloat16 [4, 3, 1024, 4096], P('dp', None, 'ctx'), may hold values from -6 to 6
- grad_y: bfloat16 [4, 1024, 4096], P('dp', 'ctx'), may hold values from -6 to 6
- short_w: float32 [7, 3, 4096], replicated, may hold values from -2 to 2
- long_h: float32 [1024, 4096], P(None, 'ctx'), may hold values from -2 to 2
- block_order: int32 [16], replicated, may hold values from 0 to 15, as said below
Outputs:
- mixed: bfloat16 [4, 1024, 4096], P('dp', 'ctx')
- feats_grad: bfloat16 [4, 3, 1024, 4096], P('dp', None, 'ctx')
- short_grad: float32 [7, 3, 4096], P(None, None, 'ctx')
- filter_grad: float32 [1024, 4096], P(None, 'ctx')
The draws below stay inside these ranges and needn't reach their ends.
Inputs may be any that keep to these rules, and one draw needn't show every extreme that they name: Stored blocks 2 i and 2 i + 1 (those of index i of ctx) hold sequence blocks i and 15 - i, in an order drawn for each i; block_order is a permutation.
All inputs are finite; a program needn't handle non-finite values.
Results may differ from the reference program's by a relative error of at most 0.0085.
Values may be sent and summed in bfloat16 or wider, within the bound.
No kernel may reach another device: no remote copies, remote signals or barrier semaphores. Data moves between devices by JAX's collectives and lax.ppermute only.
A program may use at most 192 MiB of HBM per device.

```python
import jax
import jax.numpy as jnp

D = 4096
KERNEL = 7
SEQ = 1024
BATCH = 4
BLOCKS = 16


def draw_long_h(key, part):
    key_decay, key_noise = jax.random.split(jax.random.fold_in(key, 11))
    lower_len = 16.0
    upper_len = 2.0 * SEQ
    spread = jax.random.uniform(key_decay, (1, D), jnp.float32)
    decay_len = jnp.exp(jnp.log(lower_len) + spread * (jnp.log(upper_len) - jnp.log(lower_len)))
    positions = jnp.arange(SEQ, dtype=jnp.float32)[:, None]
    amplitude = 1.0 / jnp.sqrt(jnp.minimum(decay_len, float(SEQ)))
    envelope = amplitude * jnp.exp(-positions / decay_len)
    noise_part = jnp.clip(jax.random.normal(key_noise, (SEQ, D), jnp.float32), -5.0, 5.0)
    values = envelope * noise_part
    return values.astype(jnp.float32)


def draw_block_order(key, part):
    half_count = BLOCKS // 2
    flips = jax.random.randint(jax.random.fold_in(key, 23), (half_count,), 0, 2)
    device_ids = jnp.arange(half_count, dtype=jnp.int32)
    low_ids = device_ids
    high_ids = BLOCKS - 1 - device_ids
    first_ids = jnp.where(flips == 1, high_ids, low_ids)
    second_ids = jnp.where(flips == 1, low_ids, high_ids)
    return jnp.stack([first_ids, second_ids], 1).reshape(BLOCKS).astype(jnp.int32)


def shard_levels(rng, dims, shards, low, top_value):
    def one(position, parts):
        draws = jax.random.uniform(jax.random.fold_in(jax.random.fold_in(rng, 6), position), (parts,), jnp.float32, low / len(shards), top_value / len(shards))
        return jnp.repeat(jnp.exp(draws), dims[position] // parts).reshape((-1,) + (1,) * (len(dims) - position - 1))

    level = one(*shards[0])
    for cut in shards[1:]:
        level = level * one(*cut)
    return level


def noise(own_key, shape, scale, reach, cuts=(), held_as=jnp.bfloat16):
    array = scale * jax.random.normal(own_key, shape, jnp.float32)
    if cuts:
        array = array * shard_levels(own_key, shape, cuts, -0.22, 0.18)
    return jnp.clip(array, -reach, reach).astype(held_as)


def setup_inputs(seed: int = 0) -> dict:
    key_list = jax.random.split(jax.random.key(seed), 6)
    feats = noise(key_list[0], (BATCH, 3, SEQ, D), 1.0, 6.0, ((0, 4), (2, 8)))
    grad_y = noise(key_list[1], (BATCH, SEQ, D), 1.0, 6.0, ((0, 4), (1, 8)))
    short_w = noise(key_list[2], (KERNEL, 3, D), KERNEL ** -0.5, 2.0, (), jnp.float32)
    long_h = draw_long_h(jax.random.fold_in(key_list[5], 71), 0)
    block_order = draw_block_order(jax.random.fold_in(key_list[5], 71), 0)
    return dict(feats=feats, grad_y=grad_y, short_w=short_w, long_h=long_h, block_order=block_order)


def reorder(values, table, block_count, axis):
    shape_full = values.shape
    row_total = shape_full[axis]
    grouped = values.reshape(shape_full[:axis] + (block_count, row_total // block_count) + shape_full[axis + 1:])
    return jnp.take(grouped, table, axis=axis).reshape(shape_full)


def featurize(padded, weights, rows):
    tap_count = weights.shape[0]
    total = jnp.zeros((padded.shape[0], rows, padded.shape[2]), jnp.float32)
    for offset in range(tap_count):
        begin = tap_count - 1 - offset
        total = total + weights[offset] * padded[:, begin:begin + rows].astype(jnp.float32)
    return total


def spread_back(extended, weights, rows):
    tap_count = weights.shape[0]
    total = jnp.zeros((extended.shape[0], rows, extended.shape[2]), jnp.float32)
    for offset in range(tap_count):
        total = total + weights[offset] * extended[:, offset:offset + rows]
    return total


def weight_terms(grads, padded, rows):
    tap_count = KERNEL
    terms = []
    for offset in range(tap_count):
        begin = tap_count - 1 - offset
        terms.append(jnp.sum(grads * padded[:, begin:begin + rows].astype(jnp.float32), axis=1))
    return jnp.stack(terms, 0)


def reference(feats, grad_y, short_w, long_h, block_order):
    block_count = BLOCKS
    numbers = jnp.arange(block_count, dtype=jnp.int32)
    source = jnp.sum(numbers[None, :] * (block_order[None, :] == numbers[:, None]).astype(jnp.int32), axis=1).astype(jnp.int32)
    rim_rows = KERNEL - 1
    length_full = 2 * SEQ
    tap_w = short_w[:, :, None, :]
    filter_spec = jnp.fft.rfft(long_h, n=length_full, axis=0)
    mixed_list = []
    grad_list = []
    short_total = jnp.zeros((KERNEL, 3, D), jnp.float32)
    filter_total = jnp.zeros((SEQ, D), jnp.float32)
    for seq_index in range(BATCH):
        raw_seq = reorder(feats[seq_index], source, block_count, 1)
        padded_x = jnp.concatenate([jnp.zeros((3, rim_rows, D), jnp.bfloat16), raw_seq], 1)
        featured = featurize(padded_x, tap_w, SEQ).astype(jnp.bfloat16)
        query_f = featured[0].astype(jnp.float32)
        key_part = featured[1].astype(jnp.float32)
        value_part = featured[2].astype(jnp.float32)
        gated = (key_part * value_part).astype(jnp.bfloat16)
        gated_spec = jnp.fft.rfft(gated.astype(jnp.float32), n=length_full, axis=0)
        conv_out = jnp.fft.irfft(gated_spec * filter_spec, n=length_full, axis=0)[:SEQ]
        mixed_seq = (query_f * conv_out).astype(jnp.bfloat16)
        grad_seq = reorder(grad_y[seq_index], source, block_count, 0).astype(jnp.float32)
        grad_query = (grad_seq * conv_out).astype(jnp.bfloat16)
        grad_conv = grad_seq * query_f
        back_spec = jnp.fft.rfft(grad_conv, n=length_full, axis=0)
        grad_gated = jnp.fft.irfft(back_spec * jnp.conj(filter_spec), n=length_full, axis=0)[:SEQ].astype(jnp.bfloat16)
        filter_part = jnp.fft.irfft(back_spec * jnp.conj(gated_spec), n=length_full, axis=0)[:SEQ]
        gate_grad = grad_gated.astype(jnp.float32)
        grad_feat = jnp.stack([grad_query.astype(jnp.float32), gate_grad * value_part, gate_grad * key_part], 0)
        extended = jnp.concatenate([grad_feat, jnp.zeros((3, rim_rows, D), jnp.float32)], 1)
        grad_x = spread_back(extended, tap_w, SEQ).astype(jnp.bfloat16)
        short_total = short_total + weight_terms(grad_feat, padded_x, SEQ)
        filter_total = filter_total + filter_part.astype(jnp.float32)
        mixed_list.append(reorder(mixed_seq, block_order, block_count, 0))
        grad_list.append(reorder(grad_x, block_order, block_count, 1))
    return jnp.stack(mixed_list, 0), jnp.stack(grad_list, 0), short_total, filter_total
```

```python
import functools

import jax
import jax.numpy as jnp
import ml_dtypes
import numpy as np
from jax import lax
from jax.experimental import pallas as pl
from jax.experimental.pallas import tpu as pltpu
from jax.sharding import PartitionSpec as P

BF = jnp.bfloat16
F32 = jnp.float32
RIM = 8
VMEM_BYTES = 56 * 1024 * 1024


def dft_table(size):
    freq = np.arange(size)[:, None]
    time = np.arange(size)[None, :]
    angle = (2.0 * np.pi / (2 * size)) * ((freq * time) % (2 * size))
    imag = -np.sin(angle)
    imag[0] = np.where(np.arange(size) % 2 == 0, 1.0, -1.0)
    return np.concatenate([np.cos(angle), imag], 0).astype(ml_dtypes.bfloat16)


def dot(left, right):
    return jnp.dot(left, right, preferred_element_type=F32)


def featurize_kernel(tap_count, lanes, x_ref, halo_ref, g_ref, w_ref, send_ref, qkv_ref, ext_ref):
    rows, width = g_ref.shape
    half = rows // 2
    for part in range(width // lanes):
        cols = slice(part * lanes, (part + 1) * lanes)
        for slot in range(2):
            here = slice(slot * half, (slot + 1) * half)
            made = []
            for j in range(3):
                ext = ext_ref.at[(part * 2 + slot) * 3 + j]
                ext[:RIM] = halo_ref[j, :, cols].astype(F32)[slot * RIM : (slot + 1) * RIM]
                ext[RIM:] = x_ref[j, here, cols].astype(F32)
                total = jnp.zeros((half, lanes), F32)
                for s in range(tap_count):
                    total = total + w_ref[s * 3 + j : s * 3 + j + 1, cols] * ext[RIM - s : RIM - s + half]
                made.append(total.astype(BF))
                qkv_ref[j, here, cols] = made[j]
            query, key, value = (m.astype(F32) for m in made)
            send_ref[part, 0, 0, here] = (key * value).astype(BF)
            send_ref[part, 0, 1, here] = (g_ref[here, cols].astype(F32) * query).astype(BF)


def featurize(x, halo, g, taps, tap_count, nb, n, lanes):
    rows, width = g.shape
    block = nb * lanes
    return pl.pallas_call(
        functools.partial(featurize_kernel, tap_count, lanes),
        grid=(n,),
        in_specs=[
            pl.BlockSpec((3, rows, block), lambda c: (0, 0, c)),
            pl.BlockSpec((3, 2 * RIM, block), lambda c: (0, 0, c)),
            pl.BlockSpec((rows, block), lambda c: (0, c)),
            pl.BlockSpec((taps.shape[0], block), lambda c: (0, c)),
        ],
        out_specs=[
            pl.BlockSpec((nb, 1, 2, rows, lanes), lambda c: (0, c, 0, 0, 0)),
            pl.BlockSpec((3, rows, block), lambda c: (0, 0, c)),
        ],
        out_shape=[
            jax.ShapeDtypeStruct((nb, n, 2, rows, lanes), BF),
            jax.ShapeDtypeStruct((3, rows, width), BF),
        ],
        scratch_shapes=[pltpu.VMEM((nb * 6, rows // 2 + RIM, lanes), F32)],
        compiler_params=pltpu.CompilerParams(vmem_limit_bytes=VMEM_BYTES),
    )(x, halo, g, taps)


def filter_kernel(h_ref, table_ref, out_ref):
    segments, _, size, lanes = out_ref.shape
    scale = 1.0 / size
    for s in range(segments):
        spec = dot(table_ref[...], h_ref[s * size : (s + 1) * size].astype(BF)) * scale
        first = lax.broadcasted_iota(jnp.int32, (size, lanes), 0) == 0
        real, imag = spec[:size], spec[size:]
        out_ref[s, 0] = jnp.where(first, 0.5 * real, real)
        out_ref[s, 1] = jnp.where(first, 0.0, imag)
        out_ref[s, 2] = jnp.where(first, 0.5 * imag, real)


def filter_spectrum(h, table):
    size = table.shape[1]
    segments = h.shape[0] // size
    return pl.pallas_call(
        filter_kernel,
        out_shape=jax.ShapeDtypeStruct((segments, 3, size, h.shape[1]), F32),
        compiler_params=pltpu.CompilerParams(vmem_limit_bytes=VMEM_BYTES),
    )(h, table)


def long_kernel(tile, source_ref, order_ref, recv_ref, filt_ref, table_ref, back_ref, send_ref, cross_ref,
                seq_ref, spec_ref, time_ref):
    nb, n, _, rows, lanes = recv_ref.shape
    size = table_ref.shape[1]
    segments = filt_ref.shape[0]
    half = rows // 2
    cols = nb * lanes

    def gather(p, carry):
        k = source_ref[p]
        start = pl.multiple_of((k % 2) * half, half)
        to = pl.multiple_of(p * half, half)
        for b in range(nb):
            for a in range(2):
                seq_ref[a, pl.ds(to, half), b * lanes : (b + 1) * lanes] = recv_ref[b, k // 2, a, pl.ds(start, half)]
        return carry

    lax.fori_loop(0, 2 * n, gather, 0)

    def tiled(values):
        return jnp.concatenate([values] * nb, 1) if nb > 1 else values

    def shift_sum(now, other, sign):
        return now if other is None else now + sign * other

    for step in range(size // tile):
        at = slice(step * tile, (step + 1) * tile)
        up = slice(size + step * tile, size + (step + 1) * tile)
        if step == 0:
            first = lax.broadcasted_iota(jnp.int32, (tile, cols), 0) == 0
        if segments > 1:
            sign = (1 - 2 * (lax.broadcasted_iota(jnp.int32, (tile, cols), 0) % 2)).astype(F32)
        else:
            sign = None
        gated, back, filt = [], [], []
        for s in range(segments):
            span = slice(s * size, (s + 1) * size)
            gated.append((dot(table_ref[at], seq_ref[0, span]), dot(table_ref[up], seq_ref[0, span])))
            back.append((dot(table_ref[at], seq_ref[1, span]), dot(table_ref[up], seq_ref[1, span])))
            filt.append(tuple(tiled(filt_ref[s, i, at]) for i in range(3)))

        def total(pairs, make):
            re, im = None, None
            for pair in pairs:
                a, b = make(*pair)
                re, im = (a, b) if re is None else (re + a, im + b)
            return re, im

        def through(x, f):
            return x[0] * f[0] - x[1] * f[1], x[0] * f[1] + x[1] * f[2]

        def against(x, f):
            return x[0] * f[0] + x[1] * f[1], x[1] * f[2] - x[0] * f[1]

        def triple(x):
            if step > 0:
                return x[0], x[1], x[0]
            return jnp.where(first, 0.5 * x[0], x[0]), jnp.where(first, 0.0, x[1]), jnp.where(first, 0.5 * x[1], x[0])

        triples = [triple(x) for x in gated]
        conv = [total([(gated[p - d], filt[d]) for d in range(p + 1)], through) for p in range(segments)]
        grad = [total([(back[u], filt[u - p]) for u in range(p, segments)], against) for p in range(segments)]
        cross = [total([(back[u], triples[u - p]) for u in range(p, segments)], against) for p in range(segments)]
        for p in range(segments):
            for i, rows_to in enumerate((at, up)):
                spec_ref[0, p, rows_to] = shift_sum(conv[p][i], conv[p - 1][i] if p else None, sign).astype(BF)
                ahead = p + 1 < segments
                spec_ref[1, p, rows_to] = shift_sum(grad[p][i], grad[p + 1][i] if ahead else None, sign).astype(BF)
                value = shift_sum(cross[p][i], cross[p + 1][i] if ahead else None, sign)
                summed = value[:, :lanes]
                for b in range(1, nb):
                    summed = summed + value[:, b * lanes : (b + 1) * lanes]
                cross_ref[p, rows_to] = (summed * (1.0 / size)).astype(BF)

    for a in range(2):
        time_ref[a, segments * size :] = jnp.zeros((RIM, cols), F32)
        for p in range(segments):
            for step in range(size // tile):
                at = slice(step * tile, (step + 1) * tile)
                time_ref[a, p * size + step * tile : p * size + (step + 1) * tile] = dot(back_ref[at], spec_ref[a, p])

    def scatter(i, carry):
        for a in range(2):
            starts = [pl.multiple_of(order_ref[2 * i + slot] * half, half) for slot in range(2)]
            for b in range(nb):
                lane = slice(b * lanes, (b + 1) * lanes)
                for slot in range(2):
                    send_ref[b, i, a, slot * half : (slot + 1) * half] = time_ref[a, pl.ds(starts[slot], half), lane].astype(BF)
                rims = [time_ref[a, pl.ds(pl.multiple_of(starts[slot] + half, 8), RIM), lane] for slot in range(2)]
                send_ref[b, i, a, rows:] = jnp.concatenate(rims, 0).astype(BF)
        return carry

    lax.fori_loop(0, n, scatter, 0)


def long_conv(source, order, recv, filt, table, back):
    nb, n, _, rows, lanes = recv.shape
    size = table.shape[1]
    segments = filt.shape[0]
    cols = nb * lanes
    whole = pl.BlockSpec(memory_space=pltpu.VMEM)
    scalars = pl.BlockSpec(memory_space=pltpu.SMEM)
    return pl.pallas_call(
        functools.partial(long_kernel, min(256, size)),
        in_specs=[scalars, scalars] + [whole] * 4,
        out_specs=[whole, whole],
        out_shape=[
            jax.ShapeDtypeStruct((nb, n, 2, rows + 2 * RIM, lanes), BF),
            jax.ShapeDtypeStruct((segments, 2 * size, lanes), BF),
        ],
        scratch_shapes=[
            pltpu.VMEM((2, segments * size, cols), BF),
            pltpu.VMEM((2, segments, 2 * size, cols), BF),
            pltpu.VMEM((2, segments * size + RIM, cols), F32),
        ],
        compiler_params=pltpu.CompilerParams(vmem_limit_bytes=VMEM_BYTES),
    )(source, order, recv, filt, table, back)


def filter_grad_kernel(cross_ref, back_ref, out_ref):
    size = back_ref.shape[0]
    for p in range(cross_ref.shape[0]):
        out_ref[p * size : (p + 1) * size] = dot(back_ref[...], cross_ref[p])


def filter_grad(cross, back):
    segments, _, lanes = cross.shape
    return pl.pallas_call(
        filter_grad_kernel,
        out_shape=jax.ShapeDtypeStruct((segments * back.shape[0], lanes), F32),
        compiler_params=pltpu.CompilerParams(vmem_limit_bytes=VMEM_BYTES),
    )(cross, back)


def finish_kernel(tap_count, lanes, recv_ref, qkv_ref, x_ref, g_ref, halo_ref, after_ref, w_ref,
                  mixed_ref, grad_ref, short_ref, ext_ref, gf_ref):
    rows, width = g_ref.shape
    half = rows // 2
    for part in range(width // lanes):
        cols = slice(part * lanes, (part + 1) * lanes)
        short = {}
        for slot in range(2):
            here = slice(slot * half, (slot + 1) * half)
            rim = slice(slot * RIM, (slot + 1) * RIM)

            def longer(main, after):
                return jnp.concatenate([main.astype(F32), after.astype(F32)[rim]], 0)

            conv = longer(recv_ref[part, 0, 0, here], recv_ref[part, 0, 0, rows:])
            gate = longer(recv_ref[part, 0, 1, here], recv_ref[part, 0, 1, rows:])
            key = longer(qkv_ref[1, here, cols], after_ref[0, :, cols])
            value = longer(qkv_ref[2, here, cols], after_ref[1, :, cols])
            g = longer(g_ref[here, cols], after_ref[2, :, cols])
            mixed_ref[here, cols] = (qkv_ref[0, here, cols].astype(F32) * conv[:half]).astype(BF)
            grads = ((g * conv).astype(BF).astype(F32), gate * value, gate * key)
            for j in range(3):
                ext = ext_ref.at[(part * 2 + slot) * 3 + j]
                gf = gf_ref.at[(part * 2 + slot) * 3 + j]
                ext[:RIM] = halo_ref[j, :, cols].astype(F32)[rim]
                ext[RIM:] = x_ref[j, here, cols].astype(F32)
                gf[...] = grads[j]
                total = jnp.zeros((half, lanes), F32)
                for s in range(tap_count):
                    total = total + w_ref[s * 3 + j : s * 3 + j + 1, cols] * gf[s : s + half]
                    term = grads[j][:half] * ext[RIM - s : RIM - s + half]
                    term = jnp.sum(term.reshape(half // 8, 8, lanes), 0)
                    short[s, j] = term if slot == 0 else short[s, j] + term
                grad_ref[j, here, cols] = total.astype(BF)
        for (s, j), term in short.items():
            row = s * 3 + j
            short_ref[part, 0, row : row + 1] = jnp.sum(term, 0, keepdims=True)
        used = tap_count * 3
        short_ref[part, 0, used:] = jnp.zeros((short_ref.shape[2] - used, lanes), F32)


def finish(recv, qkv, x, g, halo, after, taps, tap_count):
    nb, n, _, long_rows, lanes = recv.shape
    rows, width = g.shape
    block = nb * lanes
    short_rows = -(-tap_count * 3 // 8) * 8
    spec3 = pl.BlockSpec((3, rows, block), lambda c: (0, 0, c))
    rim3 = pl.BlockSpec((3, 2 * RIM, block), lambda c: (0, 0, c))
    flat = pl.BlockSpec((rows, block), lambda c: (0, c))
    return pl.pallas_call(
        functools.partial(finish_kernel, tap_count, lanes),
        grid=(n,),
        in_specs=[
            pl.BlockSpec((nb, 1, 2, long_rows, lanes), lambda c: (0, c, 0, 0, 0)),
            spec3, spec3, flat, rim3, rim3,
            pl.BlockSpec((taps.shape[0], block), lambda c: (0, c)),
        ],
        out_specs=[flat, spec3, pl.BlockSpec((nb, 1, short_rows, lanes), lambda c: (0, c, 0, 0))],
        out_shape=[
            jax.ShapeDtypeStruct((rows, width), BF),
            jax.ShapeDtypeStruct((3, rows, width), BF),
            jax.ShapeDtypeStruct((nb, n, short_rows, lanes), F32),
        ],
        scratch_shapes=[pltpu.VMEM((nb * 6, rows // 2 + RIM, lanes), F32)] * 2,
        compiler_params=pltpu.CompilerParams(vmem_limit_bytes=VMEM_BYTES),
    )(recv, qkv, x, g, halo, after, taps)


def on_device(feats, grad_y, short_w, long_h, block_order):
    n = lax.axis_size("ctx")
    dp = lax.axis_size("dp")
    me = lax.axis_index("ctx")
    _, _, rows, width = feats.shape
    half = rows // 2
    channels = width // n
    tap_count = short_w.shape[0]
    seq_rows = rows * n
    spread = channels % (dp * 128) == 0
    nb = dp if spread else 1
    lanes = channels // nb
    axes = ("dp", "ctx") if spread else "ctx"
    size = min(seq_rows, 1024)
    table_np = dft_table(size)
    table = jnp.asarray(table_np)
    back = jnp.asarray(np.ascontiguousarray(table_np.T))
    numbers = jnp.arange(2 * n, dtype=jnp.int32)
    source = jnp.sum(numbers[None, :] * (block_order[None, :] == numbers[:, None]).astype(jnp.int32), axis=1)
    taps = short_w.reshape(tap_count * 3, width)
    x, g = feats[0], grad_y[0]

    flip = lax.dynamic_index_in_dim(block_order, 2 * me, 0, False) != me
    upward = [(j, j + 1) for j in range(n - 1)]
    downward = [(j + 1, j) for j in range(n - 1)]
    last = me == n - 1

    def by_slot(low, high):
        return jnp.concatenate([jnp.where(flip, high, low), jnp.where(flip, low, high)], 1)

    tails = x[:, half - RIM : half], x[:, rows - RIM :]
    low_tail, high_tail = jnp.where(flip, tails[1], tails[0]), jnp.where(flip, tails[0], tails[1])
    low_before = lax.ppermute(low_tail, "ctx", upward)
    high_before = lax.ppermute(high_tail, "ctx", downward)
    halo = by_slot(low_before, jnp.where(last, low_tail, high_before))

    send, qkv = featurize(x, halo, g, taps, tap_count, nb, n, lanes)
    recv = lax.all_to_all(send.reshape((nb * n,) + send.shape[2:]), axes, 0, 0, tiled=True).reshape(send.shape)

    heads = [jnp.stack([qkv[1, r : r + RIM], qkv[2, r : r + RIM], g[r : r + RIM]], 0) for r in (0, half)]
    low_head, high_head = jnp.where(flip, heads[1], heads[0]), jnp.where(flip, heads[0], heads[1])
    low_after = lax.ppermute(low_head, "ctx", downward)
    high_after = lax.ppermute(high_head, "ctx", upward)
    after = by_slot(jnp.where(last, high_head, low_after), high_after)

    mine = lax.dynamic_slice_in_dim(long_h, lax.axis_index("dp") * lanes, lanes, 1) if spread else long_h
    filt = filter_spectrum(mine, table)
    out, cross = long_conv(source, block_order, recv, filt, table, back)
    returned = lax.all_to_all(out.reshape((nb * n,) + out.shape[2:]), axes, 0, 0, tiled=True).reshape(out.shape)
    filter_part = filter_grad(cross, back)
    if spread:
        filter_sum = lax.all_gather(filter_part, "dp", axis=1, tiled=True)
    else:
        filter_sum = lax.psum(filter_part, "dp")
    mixed, grads, short = finish(returned, qkv, x, g, halo, after, taps, tap_count)
    pieces = lax.all_to_all(short.reshape((nb * n,) + short.shape[2:]), axes, 0, 0, tiled=True)
    short_sum = jnp.sum(pieces, 0)[: tap_count * 3]
    if spread:
        short_sum = lax.all_gather(short_sum, "dp", axis=1, tiled=True)
    else:
        short_sum = lax.psum(short_sum, "dp")
    return mixed[None], grads[None], short_sum.reshape(tap_count, 3, channels), filter_sum


def solution(mesh):
    placed = (P("dp", None, "ctx", None), P("dp", "ctx", None), P(), P(None, "ctx"), P())
    return jax.shard_map(
        on_device,
        mesh=mesh,
        in_specs=placed,
        out_specs=(
            P("dp", "ctx", None),
            P("dp", None, "ctx", None),
            P(None, None, "ctx"),
            P(None, "ctx"),
        ),
        check_vma=False,
    )
```

```python
import functools

import jax
import jax.numpy as jnp
import ml_dtypes
import numpy as np
from jax import lax
from jax.experimental import pallas as pl
from jax.experimental.pallas import tpu as pltpu
from jax.sharding import PartitionSpec as P

BF = jnp.bfloat16
F32 = jnp.float32
RIM = 8
PARAMS = pltpu.CompilerParams(vmem_limit_bytes=56 * 1024 * 1024)
ANYWHERE = pl.BlockSpec(memory_space=pltpu.HBM)
VECTOR = pl.BlockSpec(memory_space=pltpu.VMEM)
SCALAR = pl.BlockSpec(memory_space=pltpu.SMEM)


def dft_tables(size):
    half = size // 2
    freq = np.arange(half)[:, None]
    tables = []
    for parity in range(2):
        time = 2 * np.arange(half)[None, :] + parity
        angle = (2.0 * np.pi / (2 * size)) * ((freq * time) % (2 * size))
        imag = -np.sin(angle)
        middle = np.pi / 2 * time[0]
        imag[0] = np.round(-np.sin(middle) if parity else np.cos(middle))
        tables.append(np.concatenate([np.cos(angle), imag], 0))
    forward = np.stack(tables).astype(ml_dtypes.bfloat16)
    return forward, np.ascontiguousarray(forward.transpose(0, 2, 1))


def dot(left, right):
    return jnp.dot(left, right, preferred_element_type=F32)


def each_part(width, body):
    lanes = min(128, width)

    def step(part, carry):
        body(pl.ds(pl.multiple_of(part * lanes, lanes), lanes))
        return carry

    lax.fori_loop(0, width // lanes, step, 0)


def chunk_at(index, channels):
    return pl.ds(pl.multiple_of(index * channels, channels), channels)


def featurize_kernel(tap_count, pieces, where_ref, x_hbm, g_hbm, halo_ref, w_ref, *refs):
    sends_hbm, qkv_hbm = refs[:pieces], refs[pieces]
    x_buf, g_buf, send_buf, qkv_buf, ext_ref, load_sem, store_sem = refs[pieces + 1 :]
    _, _, rows, channels = x_buf.shape
    half = rows // 2

    def loads(i):
        chunk = chunk_at(where_ref[i], channels)
        return [
            pltpu.make_async_copy(x_hbm.at[:, :, chunk], x_buf.at[i], load_sem.at[0, i]),
            pltpu.make_async_copy(g_hbm.at[:, chunk], g_buf.at[i], load_sem.at[1, i]),
        ]

    def stores(i):
        chunk = chunk_at(where_ref[i], channels)
        return [
            pltpu.make_async_copy(send_buf.at[i], sends_hbm[i], store_sem.at[0, i]),
            pltpu.make_async_copy(qkv_buf.at[i], qkv_hbm.at[:, :, chunk], store_sem.at[1, i]),
        ]

    for i in range(pieces):
        for copy in loads(i):
            copy.start()
    for i in range(pieces):
        for copy in loads(i):
            copy.wait()

        def body(cols):
            lanes = ext_ref.shape[-1]
            wide = pl.ds(pl.multiple_of(where_ref[i] * channels + cols.start, lanes), lanes)
            for slot in range(2):
                here = slice(slot * half, (slot + 1) * half)
                made = []
                for j in range(3):
                    ext = ext_ref.at[slot * 3 + j]
                    ext[:RIM] = halo_ref[j, :, wide].astype(F32)[slot * RIM : (slot + 1) * RIM]
                    ext[RIM:] = x_buf[i, j, here, cols].astype(F32)
                    total = jnp.zeros((half, lanes), F32)
                    for s in range(tap_count):
                        total = total + w_ref[s * 3 + j : s * 3 + j + 1, wide] * ext[RIM - s : RIM - s + half]
                    made.append(total.astype(BF))
                    qkv_buf[i, j, here, cols] = made[j]
                query, key, value = (m.astype(F32) for m in made)
                for a, sent in enumerate((key * value, g_buf[i, here, cols].astype(F32) * query)):
                    turn = ext_ref.at[slot * 3 + a, RIM:]
                    turn[...] = sent
                    for e in range(2):
                        send_buf[i, a, slot, e, :, cols] = turn[pl.ds(e, half // 2, stride=2)].astype(BF)

        each_part(channels, body)
        for copy in stores(i):
            copy.start()
    for i in range(pieces):
        for copy in stores(i):
            copy.wait()


def featurize(chunks, x, g, halo, taps, tap_count):
    rows, width = g.shape
    pieces = chunks.shape[0]
    channels = width // pieces
    *sends, qkv = pl.pallas_call(
        functools.partial(featurize_kernel, tap_count, pieces),
        in_specs=[SCALAR, ANYWHERE, ANYWHERE, VECTOR, VECTOR],
        out_specs=[ANYWHERE] * (pieces + 1),
        out_shape=[jax.ShapeDtypeStruct((2, 2, 2, rows // 4, channels), BF)] * pieces
        + [jax.ShapeDtypeStruct((3, rows, width), BF)],
        scratch_shapes=[
            pltpu.VMEM((pieces, 3, rows, channels), BF),
            pltpu.VMEM((pieces, rows, channels), BF),
            pltpu.VMEM((pieces, 2, 2, 2, rows // 4, channels), BF),
            pltpu.VMEM((pieces, 3, rows, channels), BF),
            pltpu.VMEM((6, rows // 2 + RIM, min(128, channels)), F32),
            pltpu.SemaphoreType.DMA((2, pieces)),
            pltpu.SemaphoreType.DMA((2, pieces)),
        ],
        compiler_params=PARAMS,
    )(chunks, x, g, halo, taps)
    return sends, qkv


def first_row(shape):
    return lax.broadcasted_iota(jnp.int32, shape, 0) == 0


def unite(even, odd, first):
    plus = even[0] + odd[0], even[1] + odd[1]
    minus = even[0] - odd[0], odd[1] - even[1]
    if first is not None:
        plus = plus[0], jnp.where(first, even[1], plus[1])
        minus = minus[0], jnp.where(first, odd[1], minus[1])
    return plus + minus


def divide(spec, first):
    plus_re, plus_im, minus_re, minus_im = spec
    even_im, odd_im = plus_im - minus_im, plus_im + minus_im
    if first is not None:
        even_im, odd_im = jnp.where(first, plus_im, even_im), jnp.where(first, minus_im, odd_im)
    return plus_re + minus_re, even_im, plus_re - minus_re, odd_im


def times(x, f, first, sign):
    def add(a, b):
        return a + b if sign > 0 else a - b

    out = []
    for i in (0, 2):
        re = add(x[i] * f[i], -(x[i + 1] * f[i + 1]))
        im = add(x[i + 1] * f[i], x[i] * f[i + 1])
        out += [re, im]
    if first is not None:
        middle_re = add(x[1] * f[1], -(x[3] * f[3]))
        middle_im = add(x[3] * f[1], x[1] * f[3])
        out = [
            jnp.where(first, 0.5 * (x[0] * f[0]), out[0]),
            jnp.where(first, middle_re, out[1]),
            jnp.where(first, 0.5 * (x[2] * f[2]), out[2]),
            jnp.where(first, middle_im, out[3]),
        ]
    return tuple(out)


def filter_kernel(h_ref, table_ref, out_ref, turn_ref):
    segments, _, half, width = out_ref.shape
    lanes = turn_ref.shape[-1]
    size = 2 * half
    for part in range(width // lanes):
        cols = slice(part * lanes, (part + 1) * lanes)
        turn_ref[part] = h_ref[:, cols]
        first = first_row((half, lanes))
        for s in range(segments):
            parts = []
            for e in range(2):
                time = turn_ref[part, pl.ds(s * size + e, half, stride=2)]
                made = dot(table_ref[e], time.astype(BF)) * (1.0 / size)
                parts.append((made[:half], made[half:]))
            for i, value in enumerate(unite(*parts, first)):
                out_ref[s, i, :, cols] = value


def filter_spectrum(h, table):
    size = table.shape[1]
    rows, width = h.shape
    lanes = min(128, width)
    return pl.pallas_call(
        filter_kernel,
        out_shape=jax.ShapeDtypeStruct((rows // size, 4, size // 2, width), F32),
        scratch_shapes=[pltpu.VMEM((width // lanes, rows, lanes), F32)],
        compiler_params=PARAMS,
    )(h, table)


def long_kernel(tile, n, from_ref, to_ref, filt_hbm, table_hbm, back_hbm, *refs):
    recvs_hbm, send_hbm, cross_hbm = refs[:n], refs[n], refs[n + 1]
    filt_ref, table_ref, back_ref, seq_ref, spec_ref, time_ref, cross_ref, const_sem, in_sem, out_sem = refs[n + 2 :]
    _, _, _, quarter, cols = recvs_hbm[0].shape
    _, size, freqs = table_ref.shape
    segments = filt_ref.shape[0]
    constants = [
        pltpu.make_async_copy(source, target, const_sem.at[i])
        for i, (source, target) in enumerate(((table_hbm, table_ref), (filt_hbm, filt_ref), (back_hbm, back_ref)))
    ]

    def block(position):
        return pl.ds(pl.multiple_of(position * quarter, quarter), quarter)

    arrivals = [
        pltpu.make_async_copy(
            recvs_hbm[i].at[:, slot], seq_ref.at[:, :, block(from_ref[2 * i + slot])], in_sem.at[slot, i]
        )
        for i in range(n) for slot in range(2)
    ]

    def departures(a):
        return [
            pltpu.make_async_copy(
                time_ref.at[a, :, block(to_ref[2 * i + slot])], send_hbm.at[i, a, slot], out_sem.at[a, slot, i]
            )
            for i in range(n) for slot in range(2)
        ]

    constants[0].start()
    for copy in arrivals:
        copy.start()
    constants[0].wait()
    for copy in arrivals:
        copy.wait()
    constants[1].start()
    constants[2].start()

    def total(terms):
        out = terms[0]
        for term in terms[1:]:
            out = tuple(x + y for x, y in zip(out, term))
        return out

    for step in range(freqs // tile):
        at = slice(step * tile, (step + 1) * tile)
        up = slice(freqs + step * tile, freqs + (step + 1) * tile)
        first = first_row((tile, cols)) if step == 0 else None
        sign = (1 - 2 * (lax.broadcasted_iota(jnp.int32, (tile, cols), 0) % 2)).astype(F32) if segments > 1 else None
        spectra = [[], []]
        for s in range(segments):
            span = slice(s * freqs, (s + 1) * freqs)
            for a in range(2):
                parts = [(dot(table_ref[e, at], seq_ref[a, e, span]), dot(table_ref[e, up], seq_ref[a, e, span]))
                         for e in range(2)]
                spectra[a].append(unite(*parts, first))
        if step == 0:
            constants[1].wait()
        filt = [[filt_ref[s, i, at] for i in range(4)] for s in range(segments)]
        gated, back = spectra
        conv = [total([times(gated[p - d], filt[d], first, 1) for d in range(p + 1)]) for p in range(segments)]
        grad = [total([times(back[u], filt[u - p], first, -1) for u in range(p, segments)]) for p in range(segments)]
        cross = [total([times(back[u], gated[u - p], first, -1) for u in range(p, segments)]) for p in range(segments)]

        def wrapped(values, p, other):
            if not 0 <= other < segments:
                return values[p]
            return tuple(x + sign * y for x, y in zip(values[p], values[other]))

        for p in range(segments):
            for a, value in enumerate((wrapped(conv, p, p - 1), wrapped(grad, p, p + 1))):
                for i, part in enumerate(divide(value, first)):
                    spec_ref[a, i // 2, p, at if i % 2 == 0 else up] = part.astype(BF)
            for i, part in enumerate(divide(wrapped(cross, p, p + 1), first)):
                cross_ref[p, i // 2, at if i % 2 == 0 else up] = (part * (1.0 / size)).astype(BF)

    cross_copy = pltpu.make_async_copy(cross_ref, cross_hbm, const_sem.at[0])
    cross_copy.start()
    constants[2].wait()
    for a in range(2):
        for e in range(2):
            for p in range(segments):
                for step in range(freqs // tile):
                    at = slice(step * tile, (step + 1) * tile)
                    to = slice(p * freqs + step * tile, p * freqs + (step + 1) * tile)
                    time_ref[a, e, to] = dot(back_ref[e, at], spec_ref[a, e, p]).astype(BF)
        for copy in departures(a):
            copy.start()
    for a in range(2):
        for copy in departures(a):
            copy.wait()
    cross_copy.wait()


def long_conv(come_from, go_to, recvs, filt, table, back):
    n = len(recvs)
    _, _, _, quarter, cols = recvs[0].shape
    _, size, freqs = table.shape
    segments = filt.shape[0]
    return pl.pallas_call(
        functools.partial(long_kernel, min(256, freqs), n),
        in_specs=[SCALAR, SCALAR] + [ANYWHERE] * (n + 3),
        out_specs=[ANYWHERE] * 2,
        out_shape=[
            jax.ShapeDtypeStruct((n, 2, 2, 2, quarter, cols), BF),
            jax.ShapeDtypeStruct((segments, 2, size, cols), BF),
        ],
        scratch_shapes=[
            pltpu.VMEM(filt.shape, F32),
            pltpu.VMEM(table.shape, BF),
            pltpu.VMEM(back.shape, BF),
            pltpu.VMEM((2, 2, segments * freqs, cols), BF),
            pltpu.VMEM((2, 2, segments, size, cols), BF),
            pltpu.VMEM((2, 2, segments * freqs, cols), BF),
            pltpu.VMEM((segments, 2, size, cols), BF),
            pltpu.SemaphoreType.DMA((3,)),
            pltpu.SemaphoreType.DMA((2, n)),
            pltpu.SemaphoreType.DMA((2, 2, n)),
        ],
        compiler_params=PARAMS,
    )(come_from, go_to, filt, table, back, *recvs)


def filter_grad_kernel(cross_ref, back_ref, out_ref, turn_ref):
    segments = cross_ref.shape[0]
    _, freqs, size = back_ref.shape
    parts, _, lanes = turn_ref.shape
    for p in range(segments):
        for e in range(2):
            value = dot(back_ref[e], cross_ref[p, e])
            for i in range(parts):
                turn_ref[i, pl.ds(p * size + e, freqs, stride=2)] = value[:, i * lanes : (i + 1) * lanes]
    for i in range(parts):
        out_ref[:, i * lanes : (i + 1) * lanes] = turn_ref[i].astype(BF)


def filter_grad(cross, back):
    segments, _, size, cols = cross.shape
    lanes = min(128, cols)
    return pl.pallas_call(
        filter_grad_kernel,
        out_shape=jax.ShapeDtypeStruct((segments * size, cols), BF),
        scratch_shapes=[pltpu.VMEM((cols // lanes, segments * size, lanes), F32)],
        compiler_params=PARAMS,
    )(cross, back)


def in_order(recv, a, slot, cols, turn):
    for e in range(2):
        turn[pl.ds(e, turn.shape[0] // 2, stride=2)] = recv[a, slot, e, :, cols].astype(F32)
    return turn[...]


def tap_kernel(tap_count, recv_hbm, qkv_hbm, x_hbm, g_hbm, halo_ref, short_ref, head_ref,
               recv_buf, kv_buf, x_buf, g_buf, ext_ref, turn_ref, load_sem):
    n, rows, channels = g_buf.shape
    half = rows // 2
    lanes = ext_ref.shape[-1]

    def loads(c):
        chunk = chunk_at(c, channels)
        return [
            pltpu.make_async_copy(recv_hbm.at[c], recv_buf.at[c], load_sem.at[0, c]),
            pltpu.make_async_copy(qkv_hbm.at[1:, :, chunk], kv_buf.at[c], load_sem.at[1, c]),
            pltpu.make_async_copy(x_hbm.at[:, :, chunk], x_buf.at[c], load_sem.at[2, c]),
            pltpu.make_async_copy(g_hbm.at[:, chunk], g_buf.at[c], load_sem.at[3, c]),
        ]

    for c in range(n):
        for copy in loads(c):
            copy.start()

    def one_chunk(c, carry):
        for copy in loads(c):
            copy.wait()

        def body(cols):
            wide = pl.ds(pl.multiple_of(c * channels + cols.start, lanes), lanes)
            short, heads = {}, [[], [], []]
            for slot in range(2):
                here = slice(slot * half, (slot + 1) * half)
                conv, gate = (in_order(recv_buf.at[c], a, slot, cols, turn_ref.at[slot * 2 + a]) for a in range(2))
                key, value = (kv_buf[c, j, here, cols].astype(F32) for j in range(2))
                g = g_buf[c, here, cols].astype(F32)
                grads = ((g * conv).astype(BF).astype(F32), gate * value, gate * key)
                for j in range(3):
                    ext = ext_ref.at[slot * 3 + j]
                    ext[:RIM] = halo_ref[j, :, wide].astype(F32)[slot * RIM : (slot + 1) * RIM]
                    ext[RIM:] = x_buf[c, j, here, cols].astype(F32)
                    heads[j].append(grads[j][:RIM])
                    for s in range(tap_count):
                        term = grads[j] * ext[RIM - s : RIM - s + half]
                        term = jnp.sum(term.reshape(half // 8, 8, lanes), 0)
                        short[s, j] = term if slot == 0 else short[s, j] + term
            lines = [jnp.sum(short[s, j], 0, keepdims=True) for s in range(tap_count) for j in range(3)]
            lines.append(jnp.zeros((short_ref.shape[1] - len(lines), lanes), F32))
            short_ref[c, :, cols] = jnp.concatenate(lines, 0).astype(BF)
            for j in range(3):
                head_ref[j, :, wide] = jnp.concatenate(heads[j], 0).astype(BF)

        each_part(channels, body)
        return carry

    lax.fori_loop(0, n, one_chunk, 0)


def tap_grads(recv, qkv, x, g, halo, tap_count):
    rows, width = g.shape
    n, channels = recv.shape[0], recv.shape[-1]
    lanes = min(128, channels)
    short_rows = -(-tap_count * 3 // 16) * 16
    return pl.pallas_call(
        functools.partial(tap_kernel, tap_count),
        in_specs=[ANYWHERE] * 4 + [VECTOR],
        out_specs=[VECTOR, VECTOR],
        out_shape=[
            jax.ShapeDtypeStruct((n, short_rows, channels), BF),
            jax.ShapeDtypeStruct((3, 2 * RIM, width), BF),
        ],
        scratch_shapes=[
            pltpu.VMEM(recv.shape, BF),
            pltpu.VMEM((n, 2, rows, channels), BF),
            pltpu.VMEM((n, 3, rows, channels), BF),
            pltpu.VMEM((n, rows, channels), BF),
            pltpu.VMEM((6, rows // 2 + RIM, lanes), F32),
            pltpu.VMEM((4, rows // 2, lanes), F32),
            pltpu.SemaphoreType.DMA((4, n)),
        ],
        compiler_params=PARAMS,
    )(recv, qkv, x, g, halo)


def finish_kernel(tap_count, recv_hbm, qkv_hbm, g_hbm, w_ref, mixed_hbm, grad_hbm, open_ref,
                  recv_buf, qkv_buf, g_buf, mixed_buf, grad_buf, gf_ref, turn_ref, load_sem, store_sem):
    n, rows, channels = g_buf.shape
    half = rows // 2
    lanes = gf_ref.shape[-1]

    def loads(c):
        chunk = chunk_at(c, channels)
        return [
            pltpu.make_async_copy(recv_hbm.at[c], recv_buf.at[c], load_sem.at[0, c]),
            pltpu.make_async_copy(qkv_hbm.at[:, :, chunk], qkv_buf.at[c], load_sem.at[1, c]),
            pltpu.make_async_copy(g_hbm.at[:, chunk], g_buf.at[c], load_sem.at[2, c]),
        ]

    def stores(c):
        chunk = chunk_at(c, channels)
        return [
            pltpu.make_async_copy(mixed_buf.at[c], mixed_hbm.at[:, chunk], store_sem.at[0, c]),
            pltpu.make_async_copy(grad_buf.at[c], grad_hbm.at[:, :, chunk], store_sem.at[1, c]),
        ]

    for c in range(n):
        for copy in loads(c):
            copy.start()

    def one_chunk(c, carry):
        for copy in loads(c):
            copy.wait()

        def body(cols):
            wide = pl.ds(pl.multiple_of(c * channels + cols.start, lanes), lanes)
            rest = [[], [], []]
            for slot in range(2):
                here = slice(slot * half, (slot + 1) * half)
                conv, gate = (in_order(recv_buf.at[c], a, slot, cols, turn_ref.at[slot * 2 + a]) for a in range(2))
                query, key, value = (qkv_buf[c, j, here, cols].astype(F32) for j in range(3))
                g = g_buf[c, here, cols].astype(F32)
                mixed_buf[c, here, cols] = (query * conv).astype(BF)
                grads = ((g * conv).astype(BF).astype(F32), gate * value, gate * key)
                for j in range(3):
                    gf = gf_ref.at[slot * 3 + j]
                    gf[:half] = grads[j]
                    gf[half:] = jnp.zeros((RIM, lanes), F32)
                    total = jnp.zeros((half, lanes), F32)
                    for s in range(tap_count):
                        total = total + w_ref[s * 3 + j : s * 3 + j + 1, wide] * gf[s : s + half]
                    grad_buf[c, j, here, cols] = total.astype(BF)
                    rest[j].append(total[half - RIM :])
            for j in range(3):
                open_ref[j, :, wide] = jnp.concatenate(rest[j], 0)

        each_part(channels, body)
        for copy in stores(c):
            copy.start()
        return carry

    lax.fori_loop(0, n, one_chunk, 0)
    for c in range(n):
        for copy in stores(c):
            copy.wait()


def finish(recv, qkv, g, taps, tap_count):
    rows, width = g.shape
    n, channels = recv.shape[0], recv.shape[-1]
    lanes = min(128, channels)
    return pl.pallas_call(
        functools.partial(finish_kernel, tap_count),
        in_specs=[ANYWHERE] * 3 + [VECTOR],
        out_specs=[ANYWHERE, ANYWHERE, VECTOR],
        out_shape=[
            jax.ShapeDtypeStruct((rows, width), BF),
            jax.ShapeDtypeStruct((3, rows, width), BF),
            jax.ShapeDtypeStruct((3, 2 * RIM, width), F32),
        ],
        scratch_shapes=[
            pltpu.VMEM(recv.shape, BF),
            pltpu.VMEM((n, 3, rows, channels), BF),
            pltpu.VMEM((n, rows, channels), BF),
            pltpu.VMEM((n, rows, channels), BF),
            pltpu.VMEM((n, 3, rows, channels), BF),
            pltpu.VMEM((6, rows // 2 + RIM, lanes), F32),
            pltpu.VMEM((4, rows // 2, lanes), F32),
            pltpu.SemaphoreType.DMA((3, n)),
            pltpu.SemaphoreType.DMA((2, n)),
        ],
        compiler_params=PARAMS,
    )(recv, qkv, g, taps)


def close_kernel(tap_count, old_hbm, open_ref, after_ref, w_ref, grad_hbm, tile_buf, gf_ref, load_sem, store_sem):
    rows = grad_hbm.shape[1]
    tile = 2 * RIM

    def moves(slot):
        place = grad_hbm.at[:, (slot + 1) * rows // 2 - tile : (slot + 1) * rows // 2]
        return (pltpu.make_async_copy(place, tile_buf.at[slot], load_sem.at[slot]),
                pltpu.make_async_copy(tile_buf.at[slot], place, store_sem.at[slot]))

    for slot in range(2):
        moves(slot)[0].start()
    for slot in range(2):
        moves(slot)[0].wait()

    def body(cols):
        for slot in range(2):
            rim = slice(slot * RIM, (slot + 1) * RIM)
            for j in range(3):
                gf = gf_ref.at[slot * 3 + j]
                gf[:RIM] = jnp.zeros((RIM, gf.shape[1]), F32)
                gf[RIM:] = after_ref[j, :, cols].astype(F32)[rim]
                total = open_ref[j, rim, cols]
                for s in range(1, tap_count):
                    total = total + w_ref[s * 3 + j : s * 3 + j + 1, cols] * gf[s : s + RIM]
                kept = tile_buf[slot, j, :, cols].astype(F32)[: tile - RIM]
                tile_buf[slot, j, :, cols] = jnp.concatenate([kept, total], 0).astype(BF)

    each_part(grad_hbm.shape[2], body)
    for slot in range(2):
        moves(slot)[1].start()
    for slot in range(2):
        moves(slot)[1].wait()


def close(grads, opened, after, taps, tap_count):
    width = grads.shape[2]
    return pl.pallas_call(
        functools.partial(close_kernel, tap_count),
        in_specs=[ANYWHERE, VECTOR, VECTOR, VECTOR],
        out_specs=ANYWHERE,
        out_shape=jax.ShapeDtypeStruct(grads.shape, BF),
        scratch_shapes=[
            pltpu.VMEM((2, 3, 2 * RIM, width), BF),
            pltpu.VMEM((6, 2 * RIM, min(128, width)), F32),
            pltpu.SemaphoreType.DMA((2,)),
            pltpu.SemaphoreType.DMA((2,)),
        ],
        input_output_aliases={0: 0},
        compiler_params=PARAMS,
    )(grads, opened, after, taps)


def sum_over_dp(value, keep):
    hop = 1
    total = value
    while hop < lax.axis_size("dp"):
        sent = total.astype(keep)
        other = lax.ppermute(sent, "dp", [(j, j ^ hop) for j in range(lax.axis_size("dp"))])
        total = sent.astype(F32) + other.astype(F32)
        hop *= 2
    return total


def on_device(feats, grad_y, short_w, long_h, block_order):
    n = lax.axis_size("ctx")
    me = lax.axis_index("ctx")
    _, _, rows, width = feats.shape
    half = rows // 2
    channels = width // n
    tap_count = short_w.shape[0]
    table, back = (jnp.asarray(t) for t in dft_tables(min(rows * n, 1024)))
    taps = short_w.reshape(tap_count * 3, width)
    x, g = feats[0], grad_y[0]
    numbers = jnp.arange(2 * n, dtype=jnp.int32)
    flip = jnp.sum(jnp.where(numbers == 2 * me, block_order, 0)) != me
    upward = [(j, j + 1) for j in range(n - 1)]
    downward = [(j + 1, j) for j in range(n - 1)]
    last = me == n - 1

    def by_slot(low, high):
        return jnp.concatenate([jnp.where(flip, high, low), jnp.where(flip, low, high)], 1)

    tails = x[:, half - RIM : half], x[:, rows - RIM :]
    low_tail, high_tail = jnp.where(flip, tails[1], tails[0]), jnp.where(flip, tails[0], tails[1])
    low_before = lax.ppermute(low_tail, "ctx", upward)
    high_before = lax.ppermute(high_tail, "ctx", downward)
    halo = by_slot(low_before, jnp.where(last, low_tail, high_before))
    hops = sorted(range(1, n), key=lambda s: abs(s - n // 2)) + [0]
    chunks = (me + jnp.asarray(hops, jnp.int32)) % n
    sends, qkv = featurize(chunks, x, g, halo, taps, tap_count)
    recvs = [lax.ppermute(sent, "ctx", [(j, (j + s) % n) for j in range(n)]) if s else sent
             for s, sent in zip(hops, sends)]
    long_h, qkv = lax.optimization_barrier((long_h, qkv))
    filt = filter_spectrum(long_h, table)
    origins = (me - jnp.asarray(hops, jnp.int32) + n) % n
    wanted = 2 * jnp.repeat(origins, 2) + numbers % 2
    come_from = jnp.sum(jnp.where(wanted[:, None] == numbers[None, :], block_order[None, :], 0), 1).astype(jnp.int32)
    out, cross = long_conv(come_from, block_order, recvs, filt, table, back)

    returned = lax.all_to_all(out, "ctx", 0, 0, tiled=True)
    filter_sum = sum_over_dp(filter_grad(cross, back), BF)
    returned, filter_sum = lax.optimization_barrier((returned, filter_sum))
    short, heads = tap_grads(returned, qkv, x, g, halo, tap_count)
    pieces = lax.all_to_all(short, "ctx", 0, 0, tiled=True)
    heads = heads[:, :RIM], heads[:, RIM:]
    low_head, high_head = jnp.where(flip, heads[1], heads[0]), jnp.where(flip, heads[0], heads[1])
    low_after = lax.ppermute(low_head, "ctx", downward)
    high_after = lax.ppermute(high_head, "ctx", upward)
    after = by_slot(jnp.where(last, high_head, low_after), high_after)
    mixed, grads, opened = finish(returned, qkv, g, taps, tap_count)
    grads = close(grads, opened, after, taps, tap_count)
    short_sum = sum_over_dp(jnp.sum(pieces.astype(F32), 0)[: tap_count * 3], F32)
    return mixed[None], grads[None], short_sum.reshape(tap_count, 3, channels), filter_sum


def solution(mesh):
    placed = (P("dp", None, "ctx", None), P("dp", "ctx", None), P(), P(None, "ctx"), P())
    return jax.shard_map(
        on_device,
        mesh=mesh,
        in_specs=placed,
        out_specs=(
            P("dp", "ctx", None),
            P("dp", None, "ctx", None),
            P(None, None, "ctx"),
            P(None, "ctx"),
        ),
        check_vma=False,
    )
```

```python
import functools

import jax
import jax.numpy as jnp
import ml_dtypes
import numpy as np
from jax import lax
from jax.experimental import pallas as pl
from jax.experimental.pallas import tpu as pltpu
from jax.sharding import PartitionSpec as P

BF = jnp.bfloat16
F32 = jnp.float32
RIM = 8
STRIP = 16
PARAMS = pltpu.CompilerParams(vmem_limit_bytes=63 * 1024 * 1024)
ANYWHERE = pl.BlockSpec(memory_space=pltpu.HBM)
VECTOR = pl.BlockSpec(memory_space=pltpu.VMEM)
SCALAR = pl.BlockSpec(memory_space=pltpu.SMEM)


def dft_tables(size):
    half = size // 2
    freq = np.arange(half)[:, None]
    tables = []
    for parity in range(2):
        time = 2 * np.arange(half)[None, :] + parity
        angle = (2.0 * np.pi / (2 * size)) * ((freq * time) % (2 * size))
        imag = -np.sin(angle)
        middle = np.pi / 2 * time[0]
        imag[0] = np.round(-np.sin(middle) if parity else np.cos(middle))
        tables.append(np.concatenate([np.cos(angle), imag], 0))
    forward = np.stack(tables).astype(ml_dtypes.bfloat16)
    return forward, np.ascontiguousarray(forward.transpose(0, 2, 1))


def dot(left, right):
    return jnp.dot(left, right, preferred_element_type=F32)


def each_part(width, body):
    lanes = min(128, width)

    def step(part, carry):
        body(pl.ds(pl.multiple_of(part * lanes, lanes), lanes))
        return carry

    lax.fori_loop(0, width // lanes, step, 0)


def chunk_at(index, channels):
    return pl.ds(pl.multiple_of(index * channels, channels), channels)


def featurize_kernel(tap_count, pieces, where_ref, x_hbm, g_hbm, halo_ref, w_ref, *refs):
    sends_hbm, qkv_hbm = refs[:pieces], refs[pieces]
    x_buf, g_buf, send_buf, qkv_buf, ext_ref, load_sem, store_sem = refs[pieces + 1 :]
    _, _, rows, channels = x_buf.shape
    half = rows // 2

    def loads(i):
        chunk = chunk_at(where_ref[i], channels)
        return [
            pltpu.make_async_copy(x_hbm.at[:, :, chunk], x_buf.at[i], load_sem.at[0, i]),
            pltpu.make_async_copy(g_hbm.at[:, chunk], g_buf.at[i], load_sem.at[1, i]),
        ]

    def stores(i):
        chunk = chunk_at(where_ref[i], channels)
        return [
            pltpu.make_async_copy(send_buf.at[i], sends_hbm[i], store_sem.at[0, i]),
            pltpu.make_async_copy(qkv_buf.at[i], qkv_hbm.at[:, :, chunk], store_sem.at[1, i]),
        ]

    for i in range(pieces):
        for copy in loads(i):
            copy.start()
    for i in range(pieces):
        for copy in loads(i):
            copy.wait()

        def body(cols):
            lanes = ext_ref.shape[-1]
            wide = pl.ds(pl.multiple_of(where_ref[i] * channels + cols.start, lanes), lanes)
            for slot in range(2):
                here = slice(slot * half, (slot + 1) * half)
                made = []
                for j in range(3):
                    ext = ext_ref.at[slot * 3 + j]
                    ext[:RIM] = halo_ref[j, :, wide].astype(F32)[slot * RIM : (slot + 1) * RIM]
                    ext[RIM:] = x_buf[i, j, here, cols].astype(F32)
                    total = jnp.zeros((half, lanes), F32)
                    for s in range(tap_count):
                        total = total + w_ref[s * 3 + j : s * 3 + j + 1, wide] * ext[RIM - s : RIM - s + half]
                    made.append(total.astype(BF))
                    qkv_buf[i, j, here, cols] = made[j]
                query, key, value = (m.astype(F32) for m in made)
                for a, sent in enumerate((key * value, g_buf[i, here, cols].astype(F32) * query)):
                    turn = ext_ref.at[slot * 3 + a, RIM:]
                    turn[...] = sent
                    for e in range(2):
                        send_buf[i, a, slot, e, :, cols] = turn[pl.ds(e, half // 2, stride=2)].astype(BF)

        each_part(channels, body)
        for copy in stores(i):
            copy.start()
    for i in range(pieces):
        for copy in stores(i):
            copy.wait()


def featurize(chunks, x, g, halo, taps, tap_count):
    rows, width = g.shape
    pieces = chunks.shape[0]
    channels = width // pieces
    *sends, qkv = pl.pallas_call(
        functools.partial(featurize_kernel, tap_count, pieces),
        in_specs=[SCALAR, ANYWHERE, ANYWHERE, VECTOR, VECTOR],
        out_specs=[ANYWHERE] * (pieces + 1),
        out_shape=[jax.ShapeDtypeStruct((2, 2, 2, rows // 4, channels), BF)] * pieces
        + [jax.ShapeDtypeStruct((3, rows, width), BF)],
        scratch_shapes=[
            pltpu.VMEM((pieces, 3, rows, channels), BF),
            pltpu.VMEM((pieces, rows, channels), BF),
            pltpu.VMEM((pieces, 2, 2, 2, rows // 4, channels), BF),
            pltpu.VMEM((pieces, 3, rows, channels), BF),
            pltpu.VMEM((6, rows // 2 + RIM, min(128, channels)), F32),
            pltpu.SemaphoreType.DMA((2, pieces)),
            pltpu.SemaphoreType.DMA((2, pieces)),
        ],
        compiler_params=PARAMS,
    )(chunks, x, g, halo, taps)
    return sends, qkv


def first_row(shape):
    return lax.broadcasted_iota(jnp.int32, shape, 0) == 0


def unite(even, odd, first):
    plus = even[0] + odd[0], even[1] + odd[1]
    minus = even[0] - odd[0], odd[1] - even[1]
    if first is not None:
        plus = plus[0], jnp.where(first, even[1], plus[1])
        minus = minus[0], jnp.where(first, odd[1], minus[1])
    return plus + minus


def divide(spec, first):
    plus_re, plus_im, minus_re, minus_im = spec
    even_im, odd_im = plus_im - minus_im, plus_im + minus_im
    if first is not None:
        even_im, odd_im = jnp.where(first, plus_im, even_im), jnp.where(first, minus_im, odd_im)
    return plus_re + minus_re, even_im, plus_re - minus_re, odd_im


def times(x, f, first, sign):
    def add(a, b):
        return a + b if sign > 0 else a - b

    out = []
    for i in (0, 2):
        re = add(x[i] * f[i], -(x[i + 1] * f[i + 1]))
        im = add(x[i + 1] * f[i], x[i] * f[i + 1])
        out += [re, im]
    if first is not None:
        middle_re = add(x[1] * f[1], -(x[3] * f[3]))
        middle_im = add(x[3] * f[1], x[1] * f[3])
        out = [
            jnp.where(first, 0.5 * (x[0] * f[0]), out[0]),
            jnp.where(first, middle_re, out[1]),
            jnp.where(first, 0.5 * (x[2] * f[2]), out[2]),
            jnp.where(first, middle_im, out[3]),
        ]
    return tuple(out)


def filter_kernel(h_ref, table_ref, out_ref, turn_ref):
    segments, _, half, width = out_ref.shape
    lanes = turn_ref.shape[-1]
    size = 2 * half
    for part in range(width // lanes):
        cols = slice(part * lanes, (part + 1) * lanes)
        turn_ref[part] = h_ref[:, cols]
        first = first_row((half, lanes))
        for s in range(segments):
            parts = []
            for e in range(2):
                time = turn_ref[part, pl.ds(s * size + e, half, stride=2)]
                made = dot(table_ref[e], time.astype(BF)) * (1.0 / size)
                parts.append((made[:half], made[half:]))
            for i, value in enumerate(unite(*parts, first)):
                out_ref[s, i, :, cols] = value


def filter_spectrum(h, table):
    size = table.shape[1]
    rows, width = h.shape
    lanes = min(128, width)
    return pl.pallas_call(
        filter_kernel,
        out_shape=jax.ShapeDtypeStruct((rows // size, 4, size // 2, width), F32),
        scratch_shapes=[pltpu.VMEM((width // lanes, rows, lanes), F32)],
        compiler_params=PARAMS,
    )(h, table)


def long_kernel(tile, n, from_ref, to_ref, filt_hbm, table_hbm, back_hbm, *refs):
    recvs_hbm, send_hbm, cross_hbm = refs[:n], refs[n], refs[n + 1]
    filt_ref, table_ref, back_ref, seq_ref, spec_ref, time_ref, cross_ref, mat_ref, const_sem, in_sem, out_sem = refs[n + 2 :]
    _, _, _, quarter, cols = recvs_hbm[0].shape
    _, size, freqs = table_ref.shape
    segments = filt_ref.shape[0]
    constants = [
        pltpu.make_async_copy(source, target, const_sem.at[i])
        for i, (source, target) in enumerate(((table_hbm, table_ref), (filt_hbm, filt_ref), (back_hbm, back_ref)))
    ]

    def block(position):
        return pl.ds(pl.multiple_of(position * quarter, quarter), quarter)

    arrivals = [
        pltpu.make_async_copy(
            recvs_hbm[i].at[:, slot], seq_ref.at[:, :, block(from_ref[2 * i + slot])], in_sem.at[slot, i]
        )
        for i in range(n) for slot in range(2)
    ]

    def departures(a):
        return [
            pltpu.make_async_copy(
                time_ref.at[a, :, block(to_ref[2 * i + slot])], send_hbm.at[i, a, slot], out_sem.at[a, slot, i]
            )
            for i in range(n) for slot in range(2)
        ]

    constants[0].start()
    for copy in arrivals:
        copy.start()
    constants[1].start()
    constants[2].start()
    constants[0].wait()
    for copy in arrivals:
        copy.wait()

    for a in range(2):
        for s in range(segments):
            span = slice(s * freqs, (s + 1) * freqs)
            for e in range(2):
                for step in range(size // tile):
                    at = slice(step * tile, (step + 1) * tile)
                    mat_ref[a, s, e, at] = dot(table_ref[e, at], seq_ref[a, e, span])
    constants[1].wait()

    def total(terms):
        out = terms[0]
        for term in terms[1:]:
            out = tuple(x + y for x, y in zip(out, term))
        return out

    def wrapped(values, p, other, sign):
        if not 0 <= other < segments:
            return values[p]
        return tuple(x + sign * y for x, y in zip(values[p], values[other]))

    def combine(row, lane, first):
        at, up = pl.ds(row, STRIP), pl.ds(freqs + row, STRIP)
        shape = (STRIP, lane.stop - lane.start)
        sign = (1 - 2 * (lax.broadcasted_iota(jnp.int32, shape, 0) % 2)).astype(F32) if segments > 1 else None
        first = first_row(shape) if first else None
        gated, back = (
            [unite(*((mat_ref[a, s, e, at, lane], mat_ref[a, s, e, up, lane]) for e in range(2)), first)
             for s in range(segments)]
            for a in range(2)
        )
        filt = [[filt_ref[s, i, at, lane] for i in range(4)] for s in range(segments)]
        conv = [total([times(gated[p - d], filt[d], first, 1) for d in range(p + 1)]) for p in range(segments)]
        grad = [total([times(back[u], filt[u - p], first, -1) for u in range(p, segments)]) for p in range(segments)]
        cross = [total([times(back[u], gated[u - p], first, -1) for u in range(p, segments)]) for p in range(segments)]
        for p in range(segments):
            for a, value in enumerate((wrapped(conv, p, p - 1, sign), wrapped(grad, p, p + 1, sign))):
                for i, part in enumerate(divide(value, first)):
                    spec_ref[a, i // 2, p, at if i % 2 == 0 else up, lane] = part.astype(BF)
            for i, part in enumerate(divide(wrapped(cross, p, p + 1, sign), first)):
                cross_ref[p, i // 2, at if i % 2 == 0 else up, lane] = (part * (1.0 / size)).astype(BF)

    lanes = min(128, cols)
    groups = [slice(part * lanes, (part + 1) * lanes) for part in range(cols // lanes)]

    def strip(i, carry):
        for lane in groups:
            combine(pl.multiple_of(i * STRIP, STRIP), lane, False)
        return carry

    for lane in groups:
        combine(0, lane, True)
    lax.fori_loop(1, freqs // STRIP, strip, 0)
    cross_copy = pltpu.make_async_copy(cross_ref, cross_hbm, const_sem.at[0])
    cross_copy.start()
    constants[2].wait()
    for a in range(2):
        for e in range(2):
            for p in range(segments):
                for step in range(freqs // tile):
                    at = slice(step * tile, (step + 1) * tile)
                    to = slice(p * freqs + step * tile, p * freqs + (step + 1) * tile)
                    time_ref[a, e, to] = dot(back_ref[e, at], spec_ref[a, e, p]).astype(BF)
        for copy in departures(a):
            copy.start()
    for a in range(2):
        for copy in departures(a):
            copy.wait()
    cross_copy.wait()


def long_conv(come_from, go_to, recvs, filt, table, back):
    n = len(recvs)
    _, _, _, quarter, cols = recvs[0].shape
    _, size, freqs = table.shape
    segments = filt.shape[0]
    return pl.pallas_call(
        functools.partial(long_kernel, min(256, freqs), n),
        in_specs=[SCALAR, SCALAR] + [ANYWHERE] * (n + 3),
        out_specs=[ANYWHERE] * 2,
        out_shape=[
            jax.ShapeDtypeStruct((n, 2, 2, 2, quarter, cols), BF),
            jax.ShapeDtypeStruct((segments, 2, size, cols), BF),
        ],
        scratch_shapes=[
            pltpu.VMEM(filt.shape, F32),
            pltpu.VMEM(table.shape, BF),
            pltpu.VMEM(back.shape, BF),
            pltpu.VMEM((2, 2, segments * freqs, cols), BF),
            pltpu.VMEM((2, 2, segments, size, cols), BF),
            pltpu.VMEM((2, 2, segments * freqs, cols), BF),
            pltpu.VMEM((segments, 2, size, cols), BF),
            pltpu.VMEM((2, segments, 2, size, cols), F32),
            pltpu.SemaphoreType.DMA((3,)),
            pltpu.SemaphoreType.DMA((2, n)),
            pltpu.SemaphoreType.DMA((2, 2, n)),
        ],
        compiler_params=PARAMS,
    )(come_from, go_to, filt, table, back, *recvs)


def filter_grad_kernel(cross_ref, back_ref, out_ref, turn_ref):
    segments = cross_ref.shape[0]
    _, freqs, size = back_ref.shape
    parts, _, lanes = turn_ref.shape
    for p in range(segments):
        for e in range(2):
            value = dot(back_ref[e], cross_ref[p, e])
            for i in range(parts):
                turn_ref[i, pl.ds(p * size + e, freqs, stride=2)] = value[:, i * lanes : (i + 1) * lanes]
    for i in range(parts):
        out_ref[:, i * lanes : (i + 1) * lanes] = turn_ref[i].astype(BF)


def filter_grad(cross, back):
    segments, _, size, cols = cross.shape
    lanes = min(128, cols)
    return pl.pallas_call(
        filter_grad_kernel,
        out_shape=jax.ShapeDtypeStruct((segments * size, cols), BF),
        scratch_shapes=[pltpu.VMEM((cols // lanes, segments * size, lanes), F32)],
        compiler_params=PARAMS,
    )(cross, back)


def in_order(recv, a, slot, cols, turn):
    for e in range(2):
        turn[pl.ds(e, turn.shape[0] // 2, stride=2)] = recv[a, slot, e, :, cols].astype(F32)
    return turn[...]


def tap_kernel(tap_count, recv_hbm, qkv_hbm, x_hbm, g_hbm, halo_ref, short_ref, head_ref,
               recv_buf, kv_buf, x_buf, g_buf, ext_ref, turn_ref, load_sem):
    n, rows, channels = g_buf.shape
    half = rows // 2
    lanes = ext_ref.shape[-1]

    def loads(c):
        chunk = chunk_at(c, channels)
        return [
            pltpu.make_async_copy(recv_hbm.at[c], recv_buf.at[c], load_sem.at[0, c]),
            pltpu.make_async_copy(qkv_hbm.at[1:, :, chunk], kv_buf.at[c], load_sem.at[1, c]),
            pltpu.make_async_copy(x_hbm.at[:, :, chunk], x_buf.at[c], load_sem.at[2, c]),
            pltpu.make_async_copy(g_hbm.at[:, chunk], g_buf.at[c], load_sem.at[3, c]),
        ]

    for c in range(n):
        for copy in loads(c):
            copy.start()

    def one_chunk(c, carry):
        for copy in loads(c):
            copy.wait()

        def body(cols):
            wide = pl.ds(pl.multiple_of(c * channels + cols.start, lanes), lanes)
            short, heads = {}, [[], [], []]
            for slot in range(2):
                here = slice(slot * half, (slot + 1) * half)
                conv, gate = (in_order(recv_buf.at[c], a, slot, cols, turn_ref.at[slot * 2 + a]) for a in range(2))
                key, value = (kv_buf[c, j, here, cols].astype(F32) for j in range(2))
                g = g_buf[c, here, cols].astype(F32)
                grads = ((g * conv).astype(BF).astype(F32), gate * value, gate * key)
                for j in range(3):
                    ext = ext_ref.at[slot * 3 + j]
                    ext[:RIM] = halo_ref[j, :, wide].astype(F32)[slot * RIM : (slot + 1) * RIM]
                    ext[RIM:] = x_buf[c, j, here, cols].astype(F32)
                    heads[j].append(grads[j][:RIM])
                    for s in range(tap_count):
                        term = grads[j] * ext[RIM - s : RIM - s + half]
                        term = jnp.sum(term.reshape(half // 8, 8, lanes), 0)
                        short[s, j] = term if slot == 0 else short[s, j] + term
            lines = [jnp.sum(short[s, j], 0, keepdims=True) for s in range(tap_count) for j in range(3)]
            lines.append(jnp.zeros((short_ref.shape[1] - len(lines), lanes), F32))
            short_ref[c, :, cols] = jnp.concatenate(lines, 0).astype(BF)
            for j in range(3):
                head_ref[j, :, wide] = jnp.concatenate(heads[j], 0).astype(BF)

        each_part(channels, body)
        return carry

    lax.fori_loop(0, n, one_chunk, 0)


def tap_grads(recv, qkv, x, g, halo, tap_count):
    rows, width = g.shape
    n, channels = recv.shape[0], recv.shape[-1]
    lanes = min(128, channels)
    short_rows = -(-tap_count * 3 // 16) * 16
    return pl.pallas_call(
        functools.partial(tap_kernel, tap_count),
        in_specs=[ANYWHERE] * 4 + [VECTOR],
        out_specs=[VECTOR, VECTOR],
        out_shape=[
            jax.ShapeDtypeStruct((n, short_rows, channels), BF),
            jax.ShapeDtypeStruct((3, 2 * RIM, width), BF),
        ],
        scratch_shapes=[
            pltpu.VMEM(recv.shape, BF),
            pltpu.VMEM((n, 2, rows, channels), BF),
            pltpu.VMEM((n, 3, rows, channels), BF),
            pltpu.VMEM((n, rows, channels), BF),
            pltpu.VMEM((6, rows // 2 + RIM, lanes), F32),
            pltpu.VMEM((4, rows // 2, lanes), F32),
            pltpu.SemaphoreType.DMA((4, n)),
        ],
        compiler_params=PARAMS,
    )(recv, qkv, x, g, halo)


def finish_kernel(tap_count, recv_hbm, qkv_hbm, g_hbm, w_ref, mixed_hbm, grad_hbm, open_ref,
                  recv_buf, qkv_buf, g_buf, mixed_buf, grad_buf, gf_ref, turn_ref, load_sem, store_sem):
    n, rows, channels = g_buf.shape
    half = rows // 2
    lanes = gf_ref.shape[-1]

    def loads(c):
        chunk = chunk_at(c, channels)
        return [
            pltpu.make_async_copy(recv_hbm.at[c], recv_buf.at[c], load_sem.at[0, c]),
            pltpu.make_async_copy(qkv_hbm.at[:, :, chunk], qkv_buf.at[c], load_sem.at[1, c]),
            pltpu.make_async_copy(g_hbm.at[:, chunk], g_buf.at[c], load_sem.at[2, c]),
        ]

    def stores(c):
        chunk = chunk_at(c, channels)
        return [
            pltpu.make_async_copy(mixed_buf.at[c], mixed_hbm.at[:, chunk], store_sem.at[0, c]),
            pltpu.make_async_copy(grad_buf.at[c], grad_hbm.at[:, :, chunk], store_sem.at[1, c]),
        ]

    for c in range(n):
        for copy in loads(c):
            copy.start()

    def one_chunk(c, carry):
        for copy in loads(c):
            copy.wait()

        def body(cols):
            wide = pl.ds(pl.multiple_of(c * channels + cols.start, lanes), lanes)
            rest = [[], [], []]
            for slot in range(2):
                here = slice(slot * half, (slot + 1) * half)
                conv, gate = (in_order(recv_buf.at[c], a, slot, cols, turn_ref.at[slot * 2 + a]) for a in range(2))
                query, key, value = (qkv_buf[c, j, here, cols].astype(F32) for j in range(3))
                g = g_buf[c, here, cols].astype(F32)
                mixed_buf[c, here, cols] = (query * conv).astype(BF)
                grads = ((g * conv).astype(BF).astype(F32), gate * value, gate * key)
                for j in range(3):
                    gf = gf_ref.at[slot * 3 + j]
                    gf[:half] = grads[j]
                    gf[half:] = jnp.zeros((RIM, lanes), F32)
                    total = jnp.zeros((half, lanes), F32)
                    for s in range(tap_count):
                        total = total + w_ref[s * 3 + j : s * 3 + j + 1, wide] * gf[s : s + half]
                    grad_buf[c, j, here, cols] = total.astype(BF)
                    rest[j].append(total[half - RIM :])
            for j in range(3):
                open_ref[j, :, wide] = jnp.concatenate(rest[j], 0)

        each_part(channels, body)
        for copy in stores(c):
            copy.start()
        return carry

    lax.fori_loop(0, n, one_chunk, 0)
    for c in range(n):
        for copy in stores(c):
            copy.wait()


def finish(recv, qkv, g, taps, tap_count):
    rows, width = g.shape
    n, channels = recv.shape[0], recv.shape[-1]
    lanes = min(128, channels)
    return pl.pallas_call(
        functools.partial(finish_kernel, tap_count),
        in_specs=[ANYWHERE] * 3 + [VECTOR],
        out_specs=[ANYWHERE, ANYWHERE, VECTOR],
        out_shape=[
            jax.ShapeDtypeStruct((rows, width), BF),
            jax.ShapeDtypeStruct((3, rows, width), BF),
            jax.ShapeDtypeStruct((3, 2 * RIM, width), F32),
        ],
        scratch_shapes=[
            pltpu.VMEM(recv.shape, BF),
            pltpu.VMEM((n, 3, rows, channels), BF),
            pltpu.VMEM((n, rows, channels), BF),
            pltpu.VMEM((n, rows, channels), BF),
            pltpu.VMEM((n, 3, rows, channels), BF),
            pltpu.VMEM((6, rows // 2 + RIM, lanes), F32),
            pltpu.VMEM((4, rows // 2, lanes), F32),
            pltpu.SemaphoreType.DMA((3, n)),
            pltpu.SemaphoreType.DMA((2, n)),
        ],
        compiler_params=PARAMS,
    )(recv, qkv, g, taps)


def close_kernel(tap_count, old_hbm, open_ref, after_ref, w_ref, grad_hbm, tile_buf, gf_ref, load_sem, store_sem):
    rows = grad_hbm.shape[1]
    tile = 2 * RIM

    def moves(slot):
        place = grad_hbm.at[:, (slot + 1) * rows // 2 - tile : (slot + 1) * rows // 2]
        return (pltpu.make_async_copy(place, tile_buf.at[slot], load_sem.at[slot]),
                pltpu.make_async_copy(tile_buf.at[slot], place, store_sem.at[slot]))

    for slot in range(2):
        moves(slot)[0].start()
    for slot in range(2):
        moves(slot)[0].wait()

    def body(cols):
        for slot in range(2):
            rim = slice(slot * RIM, (slot + 1) * RIM)
            for j in range(3):
                gf = gf_ref.at[slot * 3 + j]
                gf[:RIM] = jnp.zeros((RIM, gf.shape[1]), F32)
                gf[RIM:] = after_ref[j, :, cols].astype(F32)[rim]
                total = open_ref[j, rim, cols]
                for s in range(1, tap_count):
                    total = total + w_ref[s * 3 + j : s * 3 + j + 1, cols] * gf[s : s + RIM]
                kept = tile_buf[slot, j, :, cols].astype(F32)[: tile - RIM]
                tile_buf[slot, j, :, cols] = jnp.concatenate([kept, total], 0).astype(BF)

    each_part(grad_hbm.shape[2], body)
    for slot in range(2):
        moves(slot)[1].start()
    for slot in range(2):
        moves(slot)[1].wait()


def close(grads, opened, after, taps, tap_count):
    width = grads.shape[2]
    return pl.pallas_call(
        functools.partial(close_kernel, tap_count),
        in_specs=[ANYWHERE, VECTOR, VECTOR, VECTOR],
        out_specs=ANYWHERE,
        out_shape=jax.ShapeDtypeStruct(grads.shape, BF),
        scratch_shapes=[
            pltpu.VMEM((2, 3, 2 * RIM, width), BF),
            pltpu.VMEM((6, 2 * RIM, min(128, width)), F32),
            pltpu.SemaphoreType.DMA((2,)),
            pltpu.SemaphoreType.DMA((2,)),
        ],
        input_output_aliases={0: 0},
        compiler_params=PARAMS,
    )(grads, opened, after, taps)


def sum_over_dp(value, keep):
    hop = 1
    total = value
    while hop < lax.axis_size("dp"):
        sent = total.astype(keep)
        other = lax.ppermute(sent, "dp", [(j, j ^ hop) for j in range(lax.axis_size("dp"))])
        total = sent.astype(F32) + other.astype(F32)
        hop *= 2
    return total


def on_device(feats, grad_y, short_w, long_h, block_order):
    n = lax.axis_size("ctx")
    me = lax.axis_index("ctx")
    _, _, rows, width = feats.shape
    half = rows // 2
    channels = width // n
    tap_count = short_w.shape[0]
    table, back = (jnp.asarray(t) for t in dft_tables(min(rows * n, 1024)))
    taps = short_w.reshape(tap_count * 3, width)
    x, g = feats[0], grad_y[0]
    numbers = jnp.arange(2 * n, dtype=jnp.int32)
    flip = jnp.sum(jnp.where(numbers == 2 * me, block_order, 0)) != me
    upward = [(j, j + 1) for j in range(n - 1)]
    downward = [(j + 1, j) for j in range(n - 1)]
    last = me == n - 1

    def by_slot(low, high):
        return jnp.concatenate([jnp.where(flip, high, low), jnp.where(flip, low, high)], 1)

    tails = x[:, half - RIM : half], x[:, rows - RIM :]
    low_tail, high_tail = jnp.where(flip, tails[1], tails[0]), jnp.where(flip, tails[0], tails[1])
    low_before = lax.ppermute(low_tail, "ctx", upward)
    high_before = lax.ppermute(high_tail, "ctx", downward)
    halo = by_slot(low_before, jnp.where(last, low_tail, high_before))
    hops = sorted(range(1, n), key=lambda s: abs(s - n // 2)) + [0]
    chunks = (me + jnp.asarray(hops, jnp.int32)) % n
    sends, qkv = featurize(chunks, x, g, halo, taps, tap_count)
    recvs = [lax.ppermute(sent, "ctx", [(j, (j + s) % n) for j in range(n)]) if s else sent
             for s, sent in zip(hops, sends)]
    long_h, qkv = lax.optimization_barrier((long_h, qkv))
    filt = filter_spectrum(long_h, table)
    origins = (me - jnp.asarray(hops, jnp.int32) + n) % n
    wanted = 2 * jnp.repeat(origins, 2) + numbers % 2
    come_from = jnp.sum(jnp.where(wanted[:, None] == numbers[None, :], block_order[None, :], 0), 1).astype(jnp.int32)
    out, cross = long_conv(come_from, block_order, recvs, filt, table, back)

    returned = lax.all_to_all(out, "ctx", 0, 0, tiled=True)
    filter_sum = sum_over_dp(filter_grad(cross, back), BF)
    returned, filter_sum = lax.optimization_barrier((returned, filter_sum))
    short, heads = tap_grads(returned, qkv, x, g, halo, tap_count)
    pieces = lax.all_to_all(short, "ctx", 0, 0, tiled=True)
    heads = heads[:, :RIM], heads[:, RIM:]
    low_head, high_head = jnp.where(flip, heads[1], heads[0]), jnp.where(flip, heads[0], heads[1])
    low_after = lax.ppermute(low_head, "ctx", downward)
    high_after = lax.ppermute(high_head, "ctx", upward)
    after = by_slot(jnp.where(last, high_head, low_after), high_after)
    mixed, grads, opened = finish(returned, qkv, g, taps, tap_count)
    grads = close(grads, opened, after, taps, tap_count)
    short_sum = sum_over_dp(jnp.sum(pieces.astype(F32), 0)[: tap_count * 3], F32)
    return mixed[None], grads[None], short_sum.reshape(tap_count, 3, channels), filter_sum


def solution(mesh):
    placed = (P("dp", None, "ctx", None), P("dp", "ctx", None), P(), P(None, "ctx"), P())
    return jax.shard_map(
        on_device,
        mesh=mesh,
        in_specs=placed,
        out_specs=(
            P("dp", "ctx", None),
            P("dp", None, "ctx", None),
            P(None, None, "ctx"),
            P(None, "ctx"),
        ),
        check_vma=False,
    )
```

```python
import functools

import jax
import jax.numpy as jnp
import ml_dtypes
import numpy as np
from jax import lax
from jax.experimental import pallas as pl
from jax.experimental.pallas import tpu as pltpu
from jax.sharding import PartitionSpec as P

BF = jnp.bfloat16
F32 = jnp.float32
RIM = 8
STRIP = 16
UNROLL = 4
PARAMS = pltpu.CompilerParams(vmem_limit_bytes=63 * 1024 * 1024)
ANYWHERE = pl.BlockSpec(memory_space=pltpu.HBM)
VECTOR = pl.BlockSpec(memory_space=pltpu.VMEM)
SCALAR = pl.BlockSpec(memory_space=pltpu.SMEM)


def dft_tables(size):
    half = size // 2
    freq = np.arange(half)[:, None]
    tables = []
    for parity in range(2):
        time = 2 * np.arange(half)[None, :] + parity
        angle = (2.0 * np.pi / (2 * size)) * ((freq * time) % (2 * size))
        imag = -np.sin(angle)
        middle = np.pi / 2 * time[0]
        imag[0] = np.round(-np.sin(middle) if parity else np.cos(middle))
        tables.append(np.concatenate([np.cos(angle), imag], 0))
    forward = np.stack(tables).astype(ml_dtypes.bfloat16)
    return forward, np.ascontiguousarray(forward.transpose(0, 2, 1))


def dot(left, right):
    return jnp.dot(left, right, preferred_element_type=F32)


def each_part(width, body):
    lanes = min(128, width)

    def step(part, carry):
        body(pl.ds(pl.multiple_of(part * lanes, lanes), lanes))
        return carry

    lax.fori_loop(0, width // lanes, step, 0, unroll=min(UNROLL, width // lanes))


def chunk_at(index, channels):
    return pl.ds(pl.multiple_of(index * channels, channels), channels)


def featurize_kernel(tap_count, pieces, where_ref, x_hbm, g_hbm, halo_ref, w_ref, *refs):
    sends_hbm, qkv_hbm = refs[:pieces], refs[pieces]
    x_buf, g_buf, send_buf, qkv_buf, ext_ref, load_sem, store_sem = refs[pieces + 1 :]
    _, _, rows, channels = x_buf.shape
    half = rows // 2

    def loads(i):
        chunk = chunk_at(where_ref[i], channels)
        return [
            pltpu.make_async_copy(x_hbm.at[:, :, chunk], x_buf.at[i], load_sem.at[0, i]),
            pltpu.make_async_copy(g_hbm.at[:, chunk], g_buf.at[i], load_sem.at[1, i]),
        ]

    def stores(i):
        chunk = chunk_at(where_ref[i], channels)
        return [
            pltpu.make_async_copy(send_buf.at[i], sends_hbm[i], store_sem.at[0, i]),
            pltpu.make_async_copy(qkv_buf.at[i], qkv_hbm.at[:, :, chunk], store_sem.at[1, i]),
        ]

    for i in range(pieces):
        for copy in loads(i):
            copy.start()
    for i in range(pieces):
        for copy in loads(i):
            copy.wait()

        def body(cols):
            lanes = ext_ref.shape[-1]
            wide = pl.ds(pl.multiple_of(where_ref[i] * channels + cols.start, lanes), lanes)
            for slot in range(2):
                here = slice(slot * half, (slot + 1) * half)
                made = []
                for j in range(3):
                    ext = ext_ref.at[slot * 3 + j]
                    ext[:RIM] = halo_ref[j, :, wide].astype(F32)[slot * RIM : (slot + 1) * RIM]
                    ext[RIM:] = x_buf[i, j, here, cols].astype(F32)
                    total = jnp.zeros((half, lanes), F32)
                    for s in range(tap_count):
                        total = total + w_ref[s * 3 + j : s * 3 + j + 1, wide] * ext[RIM - s : RIM - s + half]
                    made.append(total.astype(BF))
                    qkv_buf[i, j, here, cols] = made[j]
                query, key, value = (m.astype(F32) for m in made)
                for a, sent in enumerate((key * value, g_buf[i, here, cols].astype(F32) * query)):
                    turn = ext_ref.at[slot * 3 + a, RIM:]
                    turn[...] = sent
                    for e in range(2):
                        send_buf[i, a, slot, e, :, cols] = turn[pl.ds(e, half // 2, stride=2)].astype(BF)

        each_part(channels, body)
        for copy in stores(i):
            copy.start()
    for i in range(pieces):
        for copy in stores(i):
            copy.wait()


def featurize(chunks, x, g, halo, taps, tap_count):
    rows, width = g.shape
    pieces = chunks.shape[0]
    channels = width // pieces
    *sends, qkv = pl.pallas_call(
        functools.partial(featurize_kernel, tap_count, pieces),
        in_specs=[SCALAR, ANYWHERE, ANYWHERE, VECTOR, VECTOR],
        out_specs=[ANYWHERE] * (pieces + 1),
        out_shape=[jax.ShapeDtypeStruct((2, 2, 2, rows // 4, channels), BF)] * pieces
        + [jax.ShapeDtypeStruct((3, rows, width), BF)],
        scratch_shapes=[
            pltpu.VMEM((pieces, 3, rows, channels), BF),
            pltpu.VMEM((pieces, rows, channels), BF),
            pltpu.VMEM((pieces, 2, 2, 2, rows // 4, channels), BF),
            pltpu.VMEM((pieces, 3, rows, channels), BF),
            pltpu.VMEM((6, rows // 2 + RIM, min(128, channels)), F32),
            pltpu.SemaphoreType.DMA((2, pieces)),
            pltpu.SemaphoreType.DMA((2, pieces)),
        ],
        compiler_params=PARAMS,
    )(chunks, x, g, halo, taps)
    return sends, qkv


def first_row(shape):
    return lax.broadcasted_iota(jnp.int32, shape, 0) == 0


def unite(even, odd, first):
    plus = even[0] + odd[0], even[1] + odd[1]
    minus = even[0] - odd[0], odd[1] - even[1]
    if first is not None:
        plus = plus[0], jnp.where(first, even[1], plus[1])
        minus = minus[0], jnp.where(first, odd[1], minus[1])
    return plus + minus


def divide(spec, first):
    plus_re, plus_im, minus_re, minus_im = spec
    even_im, odd_im = plus_im - minus_im, plus_im + minus_im
    if first is not None:
        even_im, odd_im = jnp.where(first, plus_im, even_im), jnp.where(first, minus_im, odd_im)
    return plus_re + minus_re, even_im, plus_re - minus_re, odd_im


def times(x, f, first, sign):
    def pair(x_re, x_im, f_re, f_im):
        if sign > 0:
            return x_re * f_re - x_im * f_im, x_im * f_re + x_re * f_im
        return x_re * f_re + x_im * f_im, x_im * f_re - x_re * f_im

    out = [*pair(x[0], x[1], f[0], f[1]), *pair(x[2], x[3], f[2], f[3])]
    if first is not None:
        middle_re, middle_im = pair(x[1], x[3], f[1], f[3])
        out = [
            jnp.where(first, 0.5 * (x[0] * f[0]), out[0]),
            jnp.where(first, middle_re, out[1]),
            jnp.where(first, 0.5 * (x[2] * f[2]), out[2]),
            jnp.where(first, middle_im, out[3]),
        ]
    return tuple(out)


def filter_kernel(h_ref, table_ref, out_ref, turn_ref):
    segments, _, half, width = out_ref.shape
    lanes = turn_ref.shape[-1]
    size = 2 * half
    for part in range(width // lanes):
        cols = slice(part * lanes, (part + 1) * lanes)
        turn_ref[part] = h_ref[:, cols]
        first = first_row((half, lanes))
        for s in range(segments):
            parts = []
            for e in range(2):
                time = turn_ref[part, pl.ds(s * size + e, half, stride=2)]
                made = dot(table_ref[e], time.astype(BF)) * (1.0 / size)
                parts.append((made[:half], made[half:]))
            for i, value in enumerate(unite(*parts, first)):
                out_ref[s, i, :, cols] = value


def filter_spectrum(h, table):
    size = table.shape[1]
    rows, width = h.shape
    lanes = min(128, width)
    return pl.pallas_call(
        filter_kernel,
        out_shape=jax.ShapeDtypeStruct((rows // size, 4, size // 2, width), F32),
        scratch_shapes=[pltpu.VMEM((width // lanes, rows, lanes), F32)],
        compiler_params=PARAMS,
    )(h, table)


def long_kernel(tile, n, from_ref, to_ref, filt_hbm, table_hbm, back_hbm, *refs):
    recvs_hbm, send_hbm, cross_hbm = refs[:n], refs[n], refs[n + 1]
    filt_ref, table_ref, back_ref, seq_ref, spec_ref, time_ref, cross_ref, mat_ref, const_sem, in_sem, out_sem = refs[n + 2 :]
    _, _, _, quarter, cols = recvs_hbm[0].shape
    _, size, freqs = table_ref.shape
    segments = filt_ref.shape[0]
    constants = [
        pltpu.make_async_copy(source, target, const_sem.at[i])
        for i, (source, target) in enumerate(((table_hbm, table_ref), (filt_hbm, filt_ref), (back_hbm, back_ref)))
    ]

    def block(position):
        return pl.ds(pl.multiple_of(position * quarter, quarter), quarter)

    arrivals = [
        pltpu.make_async_copy(
            recvs_hbm[i].at[:, slot], seq_ref.at[:, :, block(from_ref[2 * i + slot])], in_sem.at[slot, i]
        )
        for i in range(n) for slot in range(2)
    ]

    def departures(a):
        return [
            pltpu.make_async_copy(
                time_ref.at[a, :, block(to_ref[2 * i + slot])], send_hbm.at[i, a, slot], out_sem.at[a, slot, i]
            )
            for i in range(n) for slot in range(2)
        ]

    constants[0].start()
    for copy in arrivals:
        copy.start()
    constants[1].start()
    constants[2].start()
    constants[0].wait()
    for copy in arrivals:
        copy.wait()

    for a in range(2):
        for s in range(segments):
            span = slice(s * freqs, (s + 1) * freqs)
            for e in range(2):
                for step in range(size // tile):
                    at = slice(step * tile, (step + 1) * tile)
                    mat_ref[a, s, e, at] = dot(table_ref[e, at], seq_ref[a, e, span])
    constants[1].wait()

    def total(terms):
        out = terms[0]
        for term in terms[1:]:
            out = tuple(x + y for x, y in zip(out, term))
        return out

    def wrapped(values, p, other, sign):
        if not 0 <= other < segments:
            return values[p]
        return tuple(x + sign * y for x, y in zip(values[p], values[other]))

    def combine(row, lane, first):
        at, up = pl.ds(row, STRIP), pl.ds(freqs + row, STRIP)
        shape = (STRIP, lane.stop - lane.start)
        sign = (1 - 2 * (lax.broadcasted_iota(jnp.int32, shape, 0) % 2)).astype(F32) if segments > 1 else None
        first = first_row(shape) if first else None
        gated, back = (
            [unite(*((mat_ref[a, s, e, at, lane], mat_ref[a, s, e, up, lane]) for e in range(2)), first)
             for s in range(segments)]
            for a in range(2)
        )
        filt = [[filt_ref[s, i, at, lane] for i in range(4)] for s in range(segments)]
        conv = [total([times(gated[p - d], filt[d], first, 1) for d in range(p + 1)]) for p in range(segments)]
        grad = [total([times(back[u], filt[u - p], first, -1) for u in range(p, segments)]) for p in range(segments)]
        cross = [total([times(back[u], gated[u - p], first, -1) for u in range(p, segments)]) for p in range(segments)]
        for p in range(segments):
            for a, value in enumerate((wrapped(conv, p, p - 1, sign), wrapped(grad, p, p + 1, sign))):
                for i, part in enumerate(divide(value, first)):
                    spec_ref[a, i // 2, p, at if i % 2 == 0 else up, lane] = part.astype(BF)
            for i, part in enumerate(divide(wrapped(cross, p, p + 1, sign), first)):
                cross_ref[p, i // 2, at if i % 2 == 0 else up, lane] = part.astype(BF)

    lanes = min(128, cols)
    groups = [slice(part * lanes, (part + 1) * lanes) for part in range(cols // lanes)]

    def strip(i, carry):
        for lane in groups:
            combine(pl.multiple_of(i * STRIP, STRIP), lane, False)
        return carry

    for lane in groups:
        combine(0, lane, True)
    lax.fori_loop(1, freqs // STRIP, strip, 0)
    cross_copy = pltpu.make_async_copy(cross_ref, cross_hbm, const_sem.at[0])
    cross_copy.start()
    constants[2].wait()
    for a in range(2):
        for e in range(2):
            for p in range(segments):
                for step in range(freqs // tile):
                    at = slice(step * tile, (step + 1) * tile)
                    to = slice(p * freqs + step * tile, p * freqs + (step + 1) * tile)
                    time_ref[a, e, to] = dot(back_ref[e, at], spec_ref[a, e, p]).astype(BF)
        for copy in departures(a):
            copy.start()
    for a in range(2):
        for copy in departures(a):
            copy.wait()
    cross_copy.wait()


def long_conv(come_from, go_to, recvs, filt, table, back):
    n = len(recvs)
    _, _, _, quarter, cols = recvs[0].shape
    _, size, freqs = table.shape
    segments = filt.shape[0]
    return pl.pallas_call(
        functools.partial(long_kernel, min(256, freqs), n),
        in_specs=[SCALAR, SCALAR] + [ANYWHERE] * (n + 3),
        out_specs=[ANYWHERE] * 2,
        out_shape=[
            jax.ShapeDtypeStruct((n, 2, 2, 2, quarter, cols), BF),
            jax.ShapeDtypeStruct((segments, 2, size, cols), BF),
        ],
        scratch_shapes=[
            pltpu.VMEM(filt.shape, F32),
            pltpu.VMEM(table.shape, BF),
            pltpu.VMEM(back.shape, BF),
            pltpu.VMEM((2, 2, segments * freqs, cols), BF),
            pltpu.VMEM((2, 2, segments, size, cols), BF),
            pltpu.VMEM((2, 2, segments * freqs, cols), BF),
            pltpu.VMEM((segments, 2, size, cols), BF),
            pltpu.VMEM((2, segments, 2, size, cols), F32),
            pltpu.SemaphoreType.DMA((3,)),
            pltpu.SemaphoreType.DMA((2, n)),
            pltpu.SemaphoreType.DMA((2, 2, n)),
        ],
        compiler_params=PARAMS,
    )(come_from, go_to, filt, table, back, *recvs)


def filter_grad_kernel(cross_ref, back_ref, out_ref, turn_ref):
    segments = cross_ref.shape[0]
    _, freqs, size = back_ref.shape
    parts, _, lanes = turn_ref.shape
    for p in range(segments):
        for e in range(2):
            value = dot(back_ref[e], cross_ref[p, e]) * (1.0 / size)
            for i in range(parts):
                turn_ref[i, pl.ds(p * size + e, freqs, stride=2)] = value[:, i * lanes : (i + 1) * lanes]
    for i in range(parts):
        out_ref[:, i * lanes : (i + 1) * lanes] = turn_ref[i].astype(BF)


def filter_grad(cross, back):
    segments, _, size, cols = cross.shape
    lanes = min(128, cols)
    return pl.pallas_call(
        filter_grad_kernel,
        out_shape=jax.ShapeDtypeStruct((segments * size, cols), BF),
        scratch_shapes=[pltpu.VMEM((cols // lanes, segments * size, lanes), F32)],
        compiler_params=PARAMS,
    )(cross, back)


def in_order(recv, a, slot, cols, turn):
    for e in range(2):
        turn[pl.ds(e, turn.shape[0] // 2, stride=2)] = recv[a, slot, e, :, cols].astype(F32)
    return turn[...]


def tap_kernel(tap_count, recv_hbm, qkv_hbm, x_hbm, g_hbm, halo_ref, short_ref, head_ref,
               recv_buf, kv_buf, x_buf, g_buf, ext_ref, turn_ref, load_sem):
    n, rows, channels = g_buf.shape
    half = rows // 2
    lanes = ext_ref.shape[-1]

    def loads(c):
        chunk = chunk_at(c, channels)
        return [
            pltpu.make_async_copy(recv_hbm.at[c], recv_buf.at[c], load_sem.at[0, c]),
            pltpu.make_async_copy(qkv_hbm.at[1:, :, chunk], kv_buf.at[c], load_sem.at[1, c]),
            pltpu.make_async_copy(x_hbm.at[:, :, chunk], x_buf.at[c], load_sem.at[2, c]),
            pltpu.make_async_copy(g_hbm.at[:, chunk], g_buf.at[c], load_sem.at[3, c]),
        ]

    for c in range(n):
        for copy in loads(c):
            copy.start()

    def one_chunk(c, carry):
        for copy in loads(c):
            copy.wait()

        def body(cols):
            wide = pl.ds(pl.multiple_of(c * channels + cols.start, lanes), lanes)
            short, heads = {}, [[], [], []]
            for slot in range(2):
                here = slice(slot * half, (slot + 1) * half)
                conv, gate = (in_order(recv_buf.at[c], a, slot, cols, turn_ref.at[slot * 2 + a]) for a in range(2))
                key, value = (kv_buf[c, j, here, cols].astype(F32) for j in range(2))
                g = g_buf[c, here, cols].astype(F32)
                grads = ((g * conv).astype(BF).astype(F32), gate * value, gate * key)
                for j in range(3):
                    ext = ext_ref.at[slot * 3 + j]
                    ext[:RIM] = halo_ref[j, :, wide].astype(F32)[slot * RIM : (slot + 1) * RIM]
                    ext[RIM:] = x_buf[c, j, here, cols].astype(F32)
                    heads[j].append(grads[j][:RIM])
                    for s in range(tap_count):
                        term = grads[j] * ext[RIM - s : RIM - s + half]
                        term = jnp.sum(term.reshape(half // 8, 8, lanes), 0)
                        short[s, j] = term if slot == 0 else short[s, j] + term
            lines = [jnp.sum(short[s, j], 0, keepdims=True) for s in range(tap_count) for j in range(3)]
            lines.append(jnp.zeros((short_ref.shape[1] - len(lines), lanes), F32))
            short_ref[c, :, cols] = jnp.concatenate(lines, 0).astype(BF)
            for j in range(3):
                head_ref[j, :, wide] = jnp.concatenate(heads[j], 0).astype(BF)

        each_part(channels, body)
        return carry

    lax.fori_loop(0, n, one_chunk, 0)


def tap_grads(recv, qkv, x, g, halo, tap_count):
    rows, width = g.shape
    n, channels = recv.shape[0], recv.shape[-1]
    lanes = min(128, channels)
    short_rows = -(-tap_count * 3 // 16) * 16
    return pl.pallas_call(
        functools.partial(tap_kernel, tap_count),
        in_specs=[ANYWHERE] * 4 + [VECTOR],
        out_specs=[VECTOR, VECTOR],
        out_shape=[
            jax.ShapeDtypeStruct((n, short_rows, channels), BF),
            jax.ShapeDtypeStruct((3, 2 * RIM, width), BF),
        ],
        scratch_shapes=[
            pltpu.VMEM(recv.shape, BF),
            pltpu.VMEM((n, 2, rows, channels), BF),
            pltpu.VMEM((n, 3, rows, channels), BF),
            pltpu.VMEM((n, rows, channels), BF),
            pltpu.VMEM((6, rows // 2 + RIM, lanes), F32),
            pltpu.VMEM((4, rows // 2, lanes), F32),
            pltpu.SemaphoreType.DMA((4, n)),
        ],
        compiler_params=PARAMS,
    )(recv, qkv, x, g, halo)


def finish_kernel(tap_count, recv_hbm, qkv_hbm, g_hbm, w_ref, mixed_hbm, grad_hbm, open_ref,
                  recv_buf, qkv_buf, g_buf, mixed_buf, grad_buf, gf_ref, turn_ref, load_sem, store_sem):
    n, rows, channels = g_buf.shape
    half = rows // 2
    lanes = gf_ref.shape[-1]

    def loads(c):
        chunk = chunk_at(c, channels)
        return [
            pltpu.make_async_copy(recv_hbm.at[c], recv_buf.at[c], load_sem.at[0, c]),
            pltpu.make_async_copy(qkv_hbm.at[:, :, chunk], qkv_buf.at[c], load_sem.at[1, c]),
            pltpu.make_async_copy(g_hbm.at[:, chunk], g_buf.at[c], load_sem.at[2, c]),
        ]

    def stores(c):
        chunk = chunk_at(c, channels)
        return [
            pltpu.make_async_copy(mixed_buf.at[c], mixed_hbm.at[:, chunk], store_sem.at[0, c]),
            pltpu.make_async_copy(grad_buf.at[c], grad_hbm.at[:, :, chunk], store_sem.at[1, c]),
        ]

    for c in range(n):
        for copy in loads(c):
            copy.start()

    def one_chunk(c, carry):
        for copy in loads(c):
            copy.wait()

        def body(cols):
            wide = pl.ds(pl.multiple_of(c * channels + cols.start, lanes), lanes)
            rest = [[], [], []]
            for slot in range(2):
                here = slice(slot * half, (slot + 1) * half)
                conv, gate = (in_order(recv_buf.at[c], a, slot, cols, turn_ref.at[slot * 2 + a]) for a in range(2))
                query, key, value = (qkv_buf[c, j, here, cols].astype(F32) for j in range(3))
                g = g_buf[c, here, cols].astype(F32)
                mixed_buf[c, here, cols] = (query * conv).astype(BF)
                grads = ((g * conv).astype(BF).astype(F32), gate * value, gate * key)
                for j in range(3):
                    gf = gf_ref.at[slot * 3 + j]
                    gf[:half] = grads[j]
                    gf[half:] = jnp.zeros((RIM, lanes), F32)
                    total = jnp.zeros((half, lanes), F32)
                    for s in range(tap_count):
                        total = total + w_ref[s * 3 + j : s * 3 + j + 1, wide] * gf[s : s + half]
                    grad_buf[c, j, here, cols] = total.astype(BF)
                    rest[j].append(total[half - RIM :])
            for j in range(3):
                open_ref[j, :, wide] = jnp.concatenate(rest[j], 0)

        each_part(channels, body)
        for copy in stores(c):
            copy.start()
        return carry

    lax.fori_loop(0, n, one_chunk, 0)
    for c in range(n):
        for copy in stores(c):
            copy.wait()


def finish(recv, qkv, g, taps, tap_count):
    rows, width = g.shape
    n, channels = recv.shape[0], recv.shape[-1]
    lanes = min(128, channels)
    return pl.pallas_call(
        functools.partial(finish_kernel, tap_count),
        in_specs=[ANYWHERE] * 3 + [VECTOR],
        out_specs=[ANYWHERE, ANYWHERE, VECTOR],
        out_shape=[
            jax.ShapeDtypeStruct((rows, width), BF),
            jax.ShapeDtypeStruct((3, rows, width), BF),
            jax.ShapeDtypeStruct((3, 2 * RIM, width), F32),
        ],
        scratch_shapes=[
            pltpu.VMEM(recv.shape, BF),
            pltpu.VMEM((n, 3, rows, channels), BF),
            pltpu.VMEM((n, rows, channels), BF),
            pltpu.VMEM((n, rows, channels), BF),
            pltpu.VMEM((n, 3, rows, channels), BF),
            pltpu.VMEM((6, rows // 2 + RIM, lanes), F32),
            pltpu.VMEM((4, rows // 2, lanes), F32),
            pltpu.SemaphoreType.DMA((3, n)),
            pltpu.SemaphoreType.DMA((2, n)),
        ],
        compiler_params=PARAMS,
    )(recv, qkv, g, taps)


def swapped(order_ref):
    me = lax.axis_index("ctx")
    return ((order_ref[2 * me] != me) != (me % 2 == 1)).astype(jnp.int32)


def close_kernel(tap_count, order_ref, old_hbm, open_ref, inner_ref, outer_ref, own_ref, w_ref, grad_hbm,
                 rim_ref, tile_buf, gf_ref, load_sem, store_sem):
    rows = grad_hbm.shape[1]
    tile = 2 * RIM

    def moves(slot):
        place = grad_hbm.at[:, (slot + 1) * rows // 2 - tile : (slot + 1) * rows // 2]
        return (pltpu.make_async_copy(place, tile_buf.at[slot], load_sem.at[slot]),
                pltpu.make_async_copy(tile_buf.at[slot], place, store_sem.at[slot]))

    for slot in range(2):
        moves(slot)[0].start()
    swap = swapped(order_ref)
    last = lax.axis_index("ctx") == lax.axis_size("ctx") - 1
    rim_ref[swap] = inner_ref[...].astype(F32)
    rim_ref[1 - swap] = jnp.where(last, own_ref[...].astype(F32), outer_ref[...].astype(F32))
    for slot in range(2):
        moves(slot)[0].wait()

    def body(cols):
        for slot in range(2):
            rim = slice(slot * RIM, (slot + 1) * RIM)
            for j in range(3):
                gf = gf_ref.at[slot * 3 + j]
                gf[:RIM] = jnp.zeros((RIM, gf.shape[1]), F32)
                gf[RIM:] = rim_ref[slot, j, :, cols]
                total = open_ref[j, rim, cols]
                for s in range(1, tap_count):
                    total = total + w_ref[s * 3 + j : s * 3 + j + 1, cols] * gf[s : s + RIM]
                kept = tile_buf[slot, j, :, cols].astype(F32)[: tile - RIM]
                tile_buf[slot, j, :, cols] = jnp.concatenate([kept, total], 0).astype(BF)

    each_part(grad_hbm.shape[2], body)
    for slot in range(2):
        moves(slot)[1].start()
    for slot in range(2):
        moves(slot)[1].wait()


def close(order, grads, opened, inner, outer, own, taps, tap_count):
    width = grads.shape[2]
    return pl.pallas_call(
        functools.partial(close_kernel, tap_count),
        in_specs=[SCALAR, ANYWHERE] + [VECTOR] * 5,
        out_specs=ANYWHERE,
        out_shape=jax.ShapeDtypeStruct(grads.shape, BF),
        scratch_shapes=[
            pltpu.VMEM((2, 3, RIM, width), F32),
            pltpu.VMEM((2, 3, 2 * RIM, width), BF),
            pltpu.VMEM((6, 2 * RIM, min(128, width)), F32),
            pltpu.SemaphoreType.DMA((2,)),
            pltpu.SemaphoreType.DMA((2,)),
        ],
        input_output_aliases={1: 0},
        compiler_params=PARAMS,
    )(order, grads, opened, inner, outer, own, taps)


def sum_over_dp(value, keep):
    hop = 1
    total = value
    while hop < lax.axis_size("dp"):
        sent = total.astype(keep)
        other = lax.ppermute(sent, "dp", [(j, j ^ hop) for j in range(lax.axis_size("dp"))])
        total = sent.astype(F32) + other.astype(F32)
        hop *= 2
    return total


def on_device(feats, grad_y, short_w, long_h, block_order):
    n = lax.axis_size("ctx")
    me = lax.axis_index("ctx")
    _, _, rows, width = feats.shape
    half = rows // 2
    channels = width // n
    tap_count = short_w.shape[0]
    table, back = (jnp.asarray(t) for t in dft_tables(min(rows * n, 1024)))
    taps = short_w.reshape(tap_count * 3, width)
    x, g = feats[0], grad_y[0]
    numbers = jnp.arange(2 * n, dtype=jnp.int32)
    flip = jnp.sum(jnp.where(numbers == 2 * me, block_order, 0)) != me
    swap = flip != (me % 2 == 1)
    last = me == n - 1

    def trade(inner, outer):
        got_inner = lax.ppermute(inner, "ctx", [(j, j ^ 1) for j in range(n)])
        got_outer = lax.ppermute(outer, "ctx", [(j, j + 1 if j % 2 else j - 1) for j in range(1, n - 1)])
        return got_inner, got_outer

    tails = x[:, half - RIM : half], x[:, rows - RIM :]
    own = jnp.where(swap, tails[0], tails[1])
    inner, outer = trade(jnp.where(swap, tails[1], tails[0]), own)
    outer = jnp.where(last, own, outer)
    halo = jnp.concatenate([jnp.where(swap, inner, outer), jnp.where(swap, outer, inner)], 1)
    hops = sorted(range(1, n), key=lambda s: abs(s - n // 2)) + [0]
    chunks = (me + jnp.asarray(hops, jnp.int32)) % n
    sends, qkv = featurize(chunks, x, g, halo, taps, tap_count)
    recvs = [lax.ppermute(sent, "ctx", [(j, (j + s) % n) for j in range(n)]) if s else sent
             for s, sent in zip(hops, sends)]
    long_h, qkv = lax.optimization_barrier((long_h, qkv))
    filt = filter_spectrum(long_h, table)
    origins = (me - jnp.asarray(hops, jnp.int32) + n) % n
    wanted = 2 * jnp.repeat(origins, 2) + numbers % 2
    come_from = jnp.sum(jnp.where(wanted[:, None] == numbers[None, :], block_order[None, :], 0), 1).astype(jnp.int32)
    out, cross = long_conv(come_from, block_order, recvs, filt, table, back)

    returned = lax.all_to_all(out, "ctx", 0, 0, tiled=True)
    filter_sum = sum_over_dp(filter_grad(cross, back), BF)
    returned, filter_sum = lax.optimization_barrier((returned, filter_sum))
    short, heads = tap_grads(returned, qkv, x, g, halo, tap_count)
    pieces = lax.all_to_all(short, "ctx", 0, 0, tiled=True)
    heads = heads[:, :RIM], heads[:, RIM:]
    own = jnp.where(swap, heads[1], heads[0])
    inner, outer = trade(jnp.where(swap, heads[0], heads[1]), own)
    mixed, grads, opened = finish(returned, qkv, g, taps, tap_count)
    pieces, inner, outer, opened = lax.optimization_barrier((pieces, inner, outer, opened))
    grads = close(block_order, grads, opened, inner, outer, own, taps, tap_count)
    short_sum = sum_over_dp(jnp.sum(pieces.astype(F32), 0)[: tap_count * 3], F32)
    return mixed[None], grads[None], short_sum.reshape(tap_count, 3, channels), filter_sum


def solution(mesh):
    placed = (P("dp", None, "ctx", None), P("dp", "ctx", None), P(), P(None, "ctx"), P())
    return jax.shard_map(
        on_device,
        mesh=mesh,
        in_specs=placed,
        out_specs=(
            P("dp", "ctx", None),
            P("dp", None, "ctx", None),
            P(None, None, "ctx"),
            P(None, "ctx"),
        ),
        check_vma=False,
    )
```

```python
import functools

import jax
import jax.numpy as jnp
import ml_dtypes
import numpy as np
from jax import lax
from jax.experimental import pallas as pl
from jax.experimental.pallas import tpu as pltpu
from jax.sharding import PartitionSpec as P

BF = jnp.bfloat16
F32 = jnp.float32
RIM = 8
STRIP = 16
UNROLL = 4
PARAMS = pltpu.CompilerParams(vmem_limit_bytes=63 * 1024 * 1024)
ANYWHERE = pl.BlockSpec(memory_space=pltpu.HBM)
VECTOR = pl.BlockSpec(memory_space=pltpu.VMEM)
SCALAR = pl.BlockSpec(memory_space=pltpu.SMEM)


def dft_tables(size):
    half = size // 2
    freq = np.arange(half)[:, None]
    tables = []
    for parity in range(2):
        time = 2 * np.arange(half)[None, :] + parity
        angle = (2.0 * np.pi / (2 * size)) * ((freq * time) % (2 * size))
        imag = -np.sin(angle)
        middle = np.pi / 2 * time[0]
        imag[0] = np.round(-np.sin(middle) if parity else np.cos(middle))
        tables.append(np.concatenate([np.cos(angle), imag], 0))
    forward = np.stack(tables).astype(ml_dtypes.bfloat16)
    return forward, np.ascontiguousarray(forward.transpose(0, 2, 1))


def dot(left, right):
    return jnp.dot(left, right, preferred_element_type=F32)


def each_part(width, body):
    lanes = min(128, width)

    def step(part, carry):
        body(pl.ds(pl.multiple_of(part * lanes, lanes), lanes))
        return carry

    lax.fori_loop(0, width // lanes, step, 0, unroll=min(UNROLL, width // lanes))


def chunk_at(index, channels):
    return pl.ds(pl.multiple_of(index * channels, channels), channels)


def featurize_kernel(tap_count, pieces, where_ref, x_hbm, g_hbm, halo_ref, w_ref, *refs):
    sends_hbm, qkv_hbm = refs[:pieces], refs[pieces]
    x_buf, g_buf, send_buf, qkv_buf, ext_ref, load_sem, store_sem = refs[pieces + 1 :]
    _, _, rows, channels = x_buf.shape
    half = rows // 2

    def loads(i):
        chunk = chunk_at(where_ref[i], channels)
        return [
            pltpu.make_async_copy(x_hbm.at[:, :, chunk], x_buf.at[i], load_sem.at[0, i]),
            pltpu.make_async_copy(g_hbm.at[:, chunk], g_buf.at[i], load_sem.at[1, i]),
        ]

    def stores(i):
        chunk = chunk_at(where_ref[i], channels)
        return [
            pltpu.make_async_copy(send_buf.at[i], sends_hbm[i], store_sem.at[0, i]),
            pltpu.make_async_copy(qkv_buf.at[i], qkv_hbm.at[:, :, chunk], store_sem.at[1, i]),
        ]

    for i in range(pieces):
        for copy in loads(i):
            copy.start()
    for i in range(pieces):
        for copy in loads(i):
            copy.wait()

        def body(cols):
            lanes = ext_ref.shape[-1]
            wide = pl.ds(pl.multiple_of(where_ref[i] * channels + cols.start, lanes), lanes)
            for slot in range(2):
                here = slice(slot * half, (slot + 1) * half)
                made = []
                for j in range(3):
                    ext = ext_ref.at[slot * 3 + j]
                    ext[:RIM] = halo_ref[j, :, wide].astype(F32)[slot * RIM : (slot + 1) * RIM]
                    ext[RIM:] = x_buf[i, j, here, cols].astype(F32)
                    total = w_ref[j, :1, wide] * ext[RIM : RIM + half]
                    for s in range(1, tap_count):
                        total = total + w_ref[j, s : s + 1, wide] * ext[RIM - s : RIM - s + half]
                    made.append(total.astype(BF))
                    qkv_buf[i, j, here, cols] = made[j]
                query, key, value = (m.astype(F32) for m in made)
                for a, sent in enumerate((key * value, g_buf[i, here, cols].astype(F32) * query)):
                    turn = ext_ref.at[slot * 3 + a, RIM:]
                    turn[...] = sent
                    for e in range(2):
                        send_buf[i, a, slot, e, :, cols] = turn[pl.ds(e, half // 2, stride=2)].astype(BF)

        each_part(channels, body)
        for copy in stores(i):
            copy.start()
    for i in range(pieces):
        for copy in stores(i):
            copy.wait()


def featurize(chunks, x, g, halo, taps, tap_count):
    rows, width = g.shape
    pieces = chunks.shape[0]
    channels = width // pieces
    *sends, qkv = pl.pallas_call(
        functools.partial(featurize_kernel, tap_count, pieces),
        in_specs=[SCALAR, ANYWHERE, ANYWHERE, VECTOR, VECTOR],
        out_specs=[ANYWHERE] * (pieces + 1),
        out_shape=[jax.ShapeDtypeStruct((2, 2, 2, rows // 4, channels), BF)] * pieces
        + [jax.ShapeDtypeStruct((3, rows, width), BF)],
        scratch_shapes=[
            pltpu.VMEM((pieces, 3, rows, channels), BF),
            pltpu.VMEM((pieces, rows, channels), BF),
            pltpu.VMEM((pieces, 2, 2, 2, rows // 4, channels), BF),
            pltpu.VMEM((pieces, 3, rows, channels), BF),
            pltpu.VMEM((6, rows // 2 + RIM, min(128, channels)), F32),
            pltpu.SemaphoreType.DMA((2, pieces)),
            pltpu.SemaphoreType.DMA((2, pieces)),
        ],
        compiler_params=PARAMS,
    )(chunks, x, g, halo, taps)
    return sends, qkv


def first_row(shape):
    return lax.broadcasted_iota(jnp.int32, shape, 0) == 0


def unite(even, odd, first):
    plus = even[0] + odd[0], even[1] + odd[1]
    minus = even[0] - odd[0], odd[1] - even[1]
    if first is not None:
        plus = plus[0], jnp.where(first, even[1], plus[1])
        minus = minus[0], jnp.where(first, odd[1], minus[1])
    return plus + minus


def divide(spec, first):
    plus_re, plus_im, minus_re, minus_im = spec
    even_im, odd_im = plus_im - minus_im, plus_im + minus_im
    if first is not None:
        even_im, odd_im = jnp.where(first, plus_im, even_im), jnp.where(first, minus_im, odd_im)
    return plus_re + minus_re, even_im, plus_re - minus_re, odd_im


def times(x, f, first, sign):
    def pair(x_re, x_im, f_re, f_im):
        if sign > 0:
            return x_re * f_re - x_im * f_im, x_im * f_re + x_re * f_im
        return x_re * f_re + x_im * f_im, x_im * f_re - x_re * f_im

    out = [*pair(x[0], x[1], f[0], f[1]), *pair(x[2], x[3], f[2], f[3])]
    if first is not None:
        middle_re, middle_im = pair(x[1], x[3], f[1], f[3])
        out = [
            jnp.where(first, 0.5 * (x[0] * f[0]), out[0]),
            jnp.where(first, middle_re, out[1]),
            jnp.where(first, 0.5 * (x[2] * f[2]), out[2]),
            jnp.where(first, middle_im, out[3]),
        ]
    return tuple(out)


def filter_kernel(h_ref, table_ref, out_ref, turn_ref):
    segments, _, half, width = out_ref.shape
    lanes = turn_ref.shape[-1]
    size = 2 * half
    for part in range(width // lanes):
        cols = slice(part * lanes, (part + 1) * lanes)
        turn_ref[part] = h_ref[:, cols]
        first = first_row((half, lanes))
        for s in range(segments):
            parts = []
            for e in range(2):
                time = turn_ref[part, pl.ds(s * size + e, half, stride=2)]
                made = dot(table_ref[e], time.astype(BF)) * (1.0 / size)
                parts.append((made[:half], made[half:]))
            for i, value in enumerate(unite(*parts, first)):
                out_ref[s, i, :, cols] = value


def filter_spectrum(h, table):
    size = table.shape[1]
    rows, width = h.shape
    lanes = min(128, width)
    return pl.pallas_call(
        filter_kernel,
        out_shape=jax.ShapeDtypeStruct((rows // size, 4, size // 2, width), F32),
        scratch_shapes=[pltpu.VMEM((width // lanes, rows, lanes), F32)],
        compiler_params=PARAMS,
    )(h, table)


def long_kernel(tile, n, from_ref, to_ref, filt_hbm, table_hbm, back_hbm, *refs):
    recvs_hbm, send_hbm, cross_hbm = refs[:n], refs[n], refs[n + 1]
    filt_ref, table_ref, back_ref, seq_ref, spec_ref, time_ref, cross_ref, mat_ref, const_sem, in_sem, out_sem = refs[n + 2 :]
    _, _, _, quarter, cols = recvs_hbm[0].shape
    _, size, freqs = table_ref.shape
    segments = filt_ref.shape[0]
    constants = [
        pltpu.make_async_copy(source, target, const_sem.at[i])
        for i, (source, target) in enumerate(((table_hbm, table_ref), (filt_hbm, filt_ref), (back_hbm, back_ref)))
    ]

    def block(position):
        return pl.ds(pl.multiple_of(position * quarter, quarter), quarter)

    arrivals = [
        pltpu.make_async_copy(
            recvs_hbm[i].at[:, slot], seq_ref.at[:, :, block(from_ref[2 * i + slot])], in_sem.at[slot, i]
        )
        for i in range(n) for slot in range(2)
    ]

    def departures(a):
        return [
            pltpu.make_async_copy(
                time_ref.at[a, :, block(to_ref[2 * i + slot])], send_hbm.at[i, a, slot], out_sem.at[a, slot, i]
            )
            for i in range(n) for slot in range(2)
        ]

    constants[0].start()
    for copy in arrivals:
        copy.start()
    constants[1].start()
    constants[2].start()
    constants[0].wait()
    for copy in arrivals:
        copy.wait()

    for a in range(2):
        for s in range(segments):
            span = slice(s * freqs, (s + 1) * freqs)
            for e in range(2):
                for step in range(size // tile):
                    at = slice(step * tile, (step + 1) * tile)
                    mat_ref[a, s, e, at] = dot(table_ref[e, at], seq_ref[a, e, span])
    constants[1].wait()

    def total(terms):
        out = terms[0]
        for term in terms[1:]:
            out = tuple(x + y for x, y in zip(out, term))
        return out

    def wrapped(values, p, other, sign):
        if not 0 <= other < segments:
            return values[p]
        return tuple(x + sign * y for x, y in zip(values[p], values[other]))

    def combine(row, lane, first):
        at, up = pl.ds(row, STRIP), pl.ds(freqs + row, STRIP)
        shape = (STRIP, lane.stop - lane.start)
        sign = (1 - 2 * (lax.broadcasted_iota(jnp.int32, shape, 0) % 2)).astype(F32) if segments > 1 else None
        first = first_row(shape) if first else None
        gated, back = (
            [unite(*((mat_ref[a, s, e, at, lane], mat_ref[a, s, e, up, lane]) for e in range(2)), first)
             for s in range(segments)]
            for a in range(2)
        )
        filt = [[filt_ref[s, i, at, lane] for i in range(4)] for s in range(segments)]
        conv = [total([times(gated[p - d], filt[d], first, 1) for d in range(p + 1)]) for p in range(segments)]
        grad = [total([times(back[u], filt[u - p], first, -1) for u in range(p, segments)]) for p in range(segments)]
        cross = [total([times(back[u], gated[u - p], first, -1) for u in range(p, segments)]) for p in range(segments)]
        for p in range(segments):
            for a, value in enumerate((wrapped(conv, p, p - 1, sign), wrapped(grad, p, p + 1, sign))):
                for i, part in enumerate(divide(value, first)):
                    spec_ref[a, i // 2, p, at if i % 2 == 0 else up, lane] = part.astype(BF)
            for i, part in enumerate(divide(wrapped(cross, p, p + 1, sign), first)):
                cross_ref[p, i // 2, at if i % 2 == 0 else up, lane] = part.astype(BF)

    lanes = min(128, cols)
    groups = [slice(part * lanes, (part + 1) * lanes) for part in range(cols // lanes)]

    def strip(i, carry):
        for lane in groups:
            combine(pl.multiple_of(i * STRIP, STRIP), lane, False)
        return carry

    for lane in groups:
        combine(0, lane, True)
    lax.fori_loop(1, freqs // STRIP, strip, 0)
    cross_copy = pltpu.make_async_copy(cross_ref, cross_hbm, const_sem.at[0])
    cross_copy.start()
    constants[2].wait()
    for a in range(2):
        for e in range(2):
            for p in range(segments):
                for step in range(freqs // tile):
                    at = slice(step * tile, (step + 1) * tile)
                    to = slice(p * freqs + step * tile, p * freqs + (step + 1) * tile)
                    time_ref[a, e, to] = dot(back_ref[e, at], spec_ref[a, e, p]).astype(BF)
        for copy in departures(a):
            copy.start()
    for a in range(2):
        for copy in departures(a):
            copy.wait()
    cross_copy.wait()


def long_conv(come_from, go_to, recvs, filt, table, back):
    n = len(recvs)
    _, _, _, quarter, cols = recvs[0].shape
    _, size, freqs = table.shape
    segments = filt.shape[0]
    return pl.pallas_call(
        functools.partial(long_kernel, min(256, freqs), n),
        in_specs=[SCALAR, SCALAR] + [ANYWHERE] * (n + 3),
        out_specs=[ANYWHERE] * 2,
        out_shape=[
            jax.ShapeDtypeStruct((n, 2, 2, 2, quarter, cols), BF),
            jax.ShapeDtypeStruct((segments, 2, size, cols), BF),
        ],
        scratch_shapes=[
            pltpu.VMEM(filt.shape, F32),
            pltpu.VMEM(table.shape, BF),
            pltpu.VMEM(back.shape, BF),
            pltpu.VMEM((2, 2, segments * freqs, cols), BF),
            pltpu.VMEM((2, 2, segments, size, cols), BF),
            pltpu.VMEM((2, 2, segments * freqs, cols), BF),
            pltpu.VMEM((segments, 2, size, cols), BF),
            pltpu.VMEM((2, segments, 2, size, cols), F32),
            pltpu.SemaphoreType.DMA((3,)),
            pltpu.SemaphoreType.DMA((2, n)),
            pltpu.SemaphoreType.DMA((2, 2, n)),
        ],
        compiler_params=PARAMS,
    )(come_from, go_to, filt, table, back, *recvs)


def filter_grad_kernel(cross_ref, back_ref, out_ref, turn_ref):
    segments = cross_ref.shape[0]
    _, freqs, size = back_ref.shape
    parts, _, lanes = turn_ref.shape
    for p in range(segments):
        for e in range(2):
            value = dot(back_ref[e], cross_ref[p, e]) * (1.0 / size)
            for i in range(parts):
                turn_ref[i, pl.ds(p * size + e, freqs, stride=2)] = value[:, i * lanes : (i + 1) * lanes]
    for i in range(parts):
        out_ref[:, i * lanes : (i + 1) * lanes] = turn_ref[i].astype(BF)


def filter_grad(cross, back):
    segments, _, size, cols = cross.shape
    lanes = min(128, cols)
    return pl.pallas_call(
        filter_grad_kernel,
        out_shape=jax.ShapeDtypeStruct((segments * size, cols), BF),
        scratch_shapes=[pltpu.VMEM((cols // lanes, segments * size, lanes), F32)],
        compiler_params=PARAMS,
    )(cross, back)


def in_order(recv, a, slot, cols, turn):
    for e in range(2):
        turn[pl.ds(e, turn.shape[0] // 2, stride=2)] = recv[a, slot, e, :, cols].astype(F32)
    return turn[...]


def tap_kernel(tap_count, recv_hbm, qkv_hbm, x_hbm, g_hbm, halo_ref, short_ref, head_ref,
               recv_buf, kv_buf, x_buf, g_buf, ext_ref, turn_ref, load_sem):
    n, rows, channels = g_buf.shape
    half = rows // 2
    lanes = ext_ref.shape[-1]

    def loads(c):
        chunk = chunk_at(c, channels)
        return [
            pltpu.make_async_copy(recv_hbm.at[c], recv_buf.at[c], load_sem.at[0, c]),
            pltpu.make_async_copy(qkv_hbm.at[1:, :, chunk], kv_buf.at[c], load_sem.at[1, c]),
            pltpu.make_async_copy(x_hbm.at[:, :, chunk], x_buf.at[c], load_sem.at[2, c]),
            pltpu.make_async_copy(g_hbm.at[:, chunk], g_buf.at[c], load_sem.at[3, c]),
        ]

    for c in range(n):
        for copy in loads(c):
            copy.start()

    def one_chunk(c, carry):
        for copy in loads(c):
            copy.wait()

        def body(cols):
            wide = pl.ds(pl.multiple_of(c * channels + cols.start, lanes), lanes)
            short, heads = {}, [[], [], []]
            for slot in range(2):
                here = slice(slot * half, (slot + 1) * half)
                conv, gate = (in_order(recv_buf.at[c], a, slot, cols, turn_ref.at[slot * 2 + a]) for a in range(2))
                key, value = (kv_buf[c, j, here, cols].astype(F32) for j in range(2))
                g = g_buf[c, here, cols].astype(F32)
                grads = ((g * conv).astype(BF).astype(F32), gate * value, gate * key)
                for j in range(3):
                    ext = ext_ref.at[slot * 3 + j]
                    ext[:RIM] = halo_ref[j, :, wide].astype(F32)[slot * RIM : (slot + 1) * RIM]
                    ext[RIM:] = x_buf[c, j, here, cols].astype(F32)
                    heads[j].append(grads[j][:RIM])
                    for s in range(tap_count):
                        term = grads[j] * ext[RIM - s : RIM - s + half]
                        term = jnp.sum(term.reshape(half // 8, 8, lanes), 0)
                        short[s, j] = term if slot == 0 else short[s, j] + term
            lines = []
            for j in range(3):
                lines += [jnp.sum(short[s, j], 0, keepdims=True) for s in range(tap_count)]
                lines.append(jnp.zeros((RIM - tap_count, lanes), F32))
            lines.append(jnp.zeros((short_ref.shape[1] - 3 * RIM, lanes), F32))
            short_ref[c, :, cols] = jnp.concatenate(lines, 0).astype(BF)
            for j in range(3):
                head_ref[j, :, wide] = jnp.concatenate(heads[j], 0).astype(BF)

        each_part(channels, body)
        return carry

    lax.fori_loop(0, n, one_chunk, 0)


def tap_grads(recv, qkv, x, g, halo, tap_count):
    rows, width = g.shape
    n, channels = recv.shape[0], recv.shape[-1]
    lanes = min(128, channels)
    short_rows = -(-3 * RIM // 16) * 16
    return pl.pallas_call(
        functools.partial(tap_kernel, tap_count),
        in_specs=[ANYWHERE] * 4 + [VECTOR],
        out_specs=[VECTOR, VECTOR],
        out_shape=[
            jax.ShapeDtypeStruct((n, short_rows, channels), BF),
            jax.ShapeDtypeStruct((3, 2 * RIM, width), BF),
        ],
        scratch_shapes=[
            pltpu.VMEM(recv.shape, BF),
            pltpu.VMEM((n, 2, rows, channels), BF),
            pltpu.VMEM((n, 3, rows, channels), BF),
            pltpu.VMEM((n, rows, channels), BF),
            pltpu.VMEM((6, rows // 2 + RIM, lanes), F32),
            pltpu.VMEM((4, rows // 2, lanes), F32),
            pltpu.SemaphoreType.DMA((4, n)),
        ],
        compiler_params=PARAMS,
    )(recv, qkv, x, g, halo)


def finish_kernel(tap_count, recv_hbm, qkv_hbm, g_hbm, w_ref, mixed_hbm, grad_hbm, open_ref,
                  recv_buf, qkv_buf, g_buf, mixed_buf, grad_buf, gf_ref, turn_ref, load_sem, store_sem):
    n, rows, channels = g_buf.shape
    half = rows // 2
    lanes = gf_ref.shape[-1]

    def loads(c):
        chunk = chunk_at(c, channels)
        return [
            pltpu.make_async_copy(recv_hbm.at[c], recv_buf.at[c], load_sem.at[0, c]),
            pltpu.make_async_copy(qkv_hbm.at[:, :, chunk], qkv_buf.at[c], load_sem.at[1, c]),
            pltpu.make_async_copy(g_hbm.at[:, chunk], g_buf.at[c], load_sem.at[2, c]),
        ]

    def stores(c):
        chunk = chunk_at(c, channels)
        return [
            pltpu.make_async_copy(mixed_buf.at[c], mixed_hbm.at[:, chunk], store_sem.at[0, c]),
            pltpu.make_async_copy(grad_buf.at[c], grad_hbm.at[:, :, chunk], store_sem.at[1, c]),
        ]

    for c in range(n):
        for copy in loads(c):
            copy.start()

    def one_chunk(c, carry):
        for copy in loads(c):
            copy.wait()

        def body(cols):
            wide = pl.ds(pl.multiple_of(c * channels + cols.start, lanes), lanes)
            rest = [[], [], []]
            for slot in range(2):
                here = slice(slot * half, (slot + 1) * half)
                conv, gate = (in_order(recv_buf.at[c], a, slot, cols, turn_ref.at[slot * 2 + a]) for a in range(2))
                query, key, value = (qkv_buf[c, j, here, cols].astype(F32) for j in range(3))
                g = g_buf[c, here, cols].astype(F32)
                mixed_buf[c, here, cols] = (query * conv).astype(BF)
                grads = ((g * conv).astype(BF).astype(F32), gate * value, gate * key)
                for j in range(3):
                    gf = gf_ref.at[slot * 3 + j]
                    gf[:half] = grads[j]
                    gf[half:] = jnp.zeros((RIM, lanes), F32)
                    total = w_ref[j, :1, wide] * grads[j]
                    for s in range(1, tap_count):
                        total = total + w_ref[j, s : s + 1, wide] * gf[s : s + half]
                    grad_buf[c, j, here, cols] = total.astype(BF)
                    rest[j].append(total[half - RIM :])
            for j in range(3):
                open_ref[j, :, wide] = jnp.concatenate(rest[j], 0)

        each_part(channels, body)
        for copy in stores(c):
            copy.start()
        return carry

    lax.fori_loop(0, n, one_chunk, 0)
    for c in range(n):
        for copy in stores(c):
            copy.wait()


def finish(recv, qkv, g, taps, tap_count):
    rows, width = g.shape
    n, channels = recv.shape[0], recv.shape[-1]
    lanes = min(128, channels)
    return pl.pallas_call(
        functools.partial(finish_kernel, tap_count),
        in_specs=[ANYWHERE] * 3 + [VECTOR],
        out_specs=[ANYWHERE, ANYWHERE, VECTOR],
        out_shape=[
            jax.ShapeDtypeStruct((rows, width), BF),
            jax.ShapeDtypeStruct((3, rows, width), BF),
            jax.ShapeDtypeStruct((3, 2 * RIM, width), F32),
        ],
        scratch_shapes=[
            pltpu.VMEM(recv.shape, BF),
            pltpu.VMEM((n, 3, rows, channels), BF),
            pltpu.VMEM((n, rows, channels), BF),
            pltpu.VMEM((n, rows, channels), BF),
            pltpu.VMEM((n, 3, rows, channels), BF),
            pltpu.VMEM((6, rows // 2 + RIM, lanes), F32),
            pltpu.VMEM((4, rows // 2, lanes), F32),
            pltpu.SemaphoreType.DMA((3, n)),
            pltpu.SemaphoreType.DMA((2, n)),
        ],
        compiler_params=PARAMS,
    )(recv, qkv, g, taps)


def swapped(order_ref):
    me = lax.axis_index("ctx")
    return ((order_ref[2 * me] != me) != (me % 2 == 1)).astype(jnp.int32)


def close_kernel(tap_count, order_ref, old_hbm, open_ref, inner_ref, outer_ref, own_ref, w_ref, grad_hbm,
                 rim_ref, tile_buf, gf_ref, load_sem, store_sem):
    rows = grad_hbm.shape[1]
    tile = 2 * RIM

    def place(slot):
        return grad_hbm.at[:, (slot + 1) * rows // 2 - tile : (slot + 1) * rows // 2]

    def load(slot):
        return pltpu.make_async_copy(place(slot), tile_buf.at[slot], load_sem.at[slot])

    def store(slot):
        return pltpu.make_async_copy(tile_buf.at[slot], place(slot), store_sem.at[slot])

    for slot in range(2):
        load(slot).start()
    swap = swapped(order_ref)
    last = lax.axis_index("ctx") == lax.axis_size("ctx") - 1
    rim_ref[swap] = inner_ref[...].astype(F32)
    rim_ref[1 - swap] = jnp.where(last, own_ref[...].astype(F32), outer_ref[...].astype(F32))
    for slot in range(2):
        load(slot).wait()

    def body(cols):
        for slot in range(2):
            rim = slice(slot * RIM, (slot + 1) * RIM)
            for j in range(3):
                gf = gf_ref.at[slot * 3 + j]
                gf[:RIM] = jnp.zeros((RIM, gf.shape[1]), F32)
                gf[RIM:] = rim_ref[slot, j, :, cols]
                total = open_ref[j, rim, cols]
                for s in range(1, tap_count):
                    total = total + w_ref[j, s : s + 1, cols] * gf[s : s + RIM]
                kept = tile_buf[slot, j, :, cols].astype(F32)[: tile - RIM]
                tile_buf[slot, j, :, cols] = jnp.concatenate([kept, total], 0).astype(BF)

    each_part(grad_hbm.shape[2], body)
    for slot in range(2):
        store(slot).start()
    for slot in range(2):
        store(slot).wait()


def close(order, grads, opened, inner, outer, own, taps, tap_count):
    width = grads.shape[2]
    return pl.pallas_call(
        functools.partial(close_kernel, tap_count),
        in_specs=[SCALAR, ANYWHERE] + [VECTOR] * 5,
        out_specs=ANYWHERE,
        out_shape=jax.ShapeDtypeStruct(grads.shape, BF),
        scratch_shapes=[
            pltpu.VMEM((2, 3, RIM, width), F32),
            pltpu.VMEM((2, 3, 2 * RIM, width), BF),
            pltpu.VMEM((6, 2 * RIM, min(128, width)), F32),
            pltpu.SemaphoreType.DMA((2,)),
            pltpu.SemaphoreType.DMA((2,)),
        ],
        input_output_aliases={1: 0},
        compiler_params=PARAMS,
    )(order, grads, opened, inner, outer, own, taps)


def sum_over_dp(value, keep):
    hop = 1
    total = value
    while hop < lax.axis_size("dp"):
        sent = total.astype(keep)
        other = lax.ppermute(sent, "dp", [(j, j ^ hop) for j in range(lax.axis_size("dp"))])
        total = sent.astype(F32) + other.astype(F32)
        hop *= 2
    return total


def on_device(feats, grad_y, short_w, long_h, block_order):
    n = lax.axis_size("ctx")
    me = lax.axis_index("ctx")
    _, _, rows, width = feats.shape
    half = rows // 2
    channels = width // n
    tap_count = short_w.shape[0]
    table, back = (jnp.asarray(t) for t in dft_tables(min(rows * n, 1024)))
    taps = short_w.transpose(1, 0, 2)
    x, g = feats[0], grad_y[0]
    numbers = jnp.arange(2 * n, dtype=jnp.int32)
    flip = jnp.sum(jnp.where(numbers == 2 * me, block_order, 0)) != me
    swap = flip != (me % 2 == 1)
    last = me == n - 1

    def trade(inner, outer):
        got_inner = lax.ppermute(inner, "ctx", [(j, j ^ 1) for j in range(n)])
        got_outer = lax.ppermute(outer, "ctx", [(j, j + 1 if j % 2 else j - 1) for j in range(1, n - 1)])
        return got_inner, got_outer

    tails = x[:, half - RIM : half], x[:, rows - RIM :]
    own = jnp.where(swap, tails[0], tails[1])
    inner, outer = trade(jnp.where(swap, tails[1], tails[0]), own)
    outer = jnp.where(last, own, outer)
    halo = jnp.concatenate([jnp.where(swap, inner, outer), jnp.where(swap, outer, inner)], 1)
    hops = sorted(range(1, n), key=lambda s: (s != 2, abs(s - n // 2))) + [0]
    chunks = (me + jnp.asarray(hops, jnp.int32)) % n
    sends, qkv = featurize(chunks, x, g, halo, taps, tap_count)
    recvs = [lax.ppermute(sent, "ctx", [(j, (j + s) % n) for j in range(n)]) if s else sent
             for s, sent in zip(hops, sends)]
    long_h, qkv = lax.optimization_barrier((long_h, qkv))
    filt = filter_spectrum(long_h, table)
    origins = (me - jnp.asarray(hops, jnp.int32) + n) % n
    wanted = 2 * jnp.repeat(origins, 2) + numbers % 2
    come_from = jnp.sum(jnp.where(wanted[:, None] == numbers[None, :], block_order[None, :], 0), 1).astype(jnp.int32)
    out, cross = long_conv(come_from, block_order, recvs, filt, table, back)

    returned = lax.all_to_all(out, "ctx", 0, 0, tiled=True)
    filter_sum = sum_over_dp(filter_grad(cross, back), BF)
    returned, filter_sum = lax.optimization_barrier((returned, filter_sum))
    short, heads = tap_grads(returned, qkv, x, g, halo, tap_count)
    pieces = lax.all_to_all(short, "ctx", 0, 0, tiled=True)
    heads = heads[:, :RIM], heads[:, RIM:]
    own = jnp.where(swap, heads[1], heads[0])
    inner, outer = trade(jnp.where(swap, heads[0], heads[1]), own)
    mixed, grads, opened = finish(returned, qkv, g, taps, tap_count)
    pieces, inner, outer, opened = lax.optimization_barrier((pieces, inner, outer, opened))
    grads = close(block_order, grads, opened, inner, outer, own, taps, tap_count)
    short_sum = sum_over_dp(jnp.sum(pieces.astype(F32), 0)[: 3 * RIM], F32)
    short_sum = short_sum.reshape(3, RIM, channels)[:, :tap_count].transpose(1, 0, 2)
    return mixed[None], grads[None], short_sum, filter_sum


def solution(mesh):
    placed = (P("dp", None, "ctx", None), P("dp", "ctx", None), P(), P(None, "ctx"), P())
    return jax.shard_map(
        on_device,
        mesh=mesh,
        in_specs=placed,
        out_specs=(
            P("dp", "ctx", None),
            P("dp", None, "ctx", None),
            P(None, None, "ctx"),
            P(None, "ctx"),
        ),
        check_vma=False,
    )
```

```python
import functools

import jax
import jax.numpy as jnp
import ml_dtypes
import numpy as np
from jax import lax
from jax.experimental import pallas as pl
from jax.experimental.pallas import tpu as pltpu
from jax.sharding import PartitionSpec as P

BF = jnp.bfloat16
F32 = jnp.float32
RIM = 8
STRIP = 16
UNROLL = 4
PARAMS = pltpu.CompilerParams(vmem_limit_bytes=63 * 1024 * 1024)
ANYWHERE = pl.BlockSpec(memory_space=pltpu.HBM)
VECTOR = pl.BlockSpec(memory_space=pltpu.VMEM)
SCALAR = pl.BlockSpec(memory_space=pltpu.SMEM)


def dft_tables(size):
    half = size // 2
    freq = np.arange(half)[:, None]
    tables = []
    for parity in range(2):
        time = 2 * np.arange(half)[None, :] + parity
        angle = (2.0 * np.pi / (2 * size)) * ((freq * time) % (2 * size))
        imag = -np.sin(angle)
        middle = np.pi / 2 * time[0]
        imag[0] = np.round(-np.sin(middle) if parity else np.cos(middle))
        tables.append(np.concatenate([np.cos(angle), imag], 0))
    forward = np.stack(tables).astype(ml_dtypes.bfloat16)
    return forward, np.ascontiguousarray(forward.transpose(0, 2, 1))


def dot(left, right):
    return jnp.dot(left, right, preferred_element_type=F32)


def each_part(width, body):
    lanes = min(128, width)

    def step(part, carry):
        body(pl.ds(pl.multiple_of(part * lanes, lanes), lanes))
        return carry

    lax.fori_loop(0, width // lanes, step, 0, unroll=min(UNROLL, width // lanes))


def chunk_at(index, channels):
    return pl.ds(pl.multiple_of(index * channels, channels), channels)


def featurize_kernel(tap_count, pieces, where_ref, x_hbm, g_hbm, halo_ref, w_ref, *refs):
    sends_hbm, qkv_hbm = refs[:pieces], refs[pieces]
    x_buf, g_buf, send_buf, qkv_buf, ext_ref, load_sem, store_sem = refs[pieces + 1 :]
    _, _, rows, channels = x_buf.shape
    half = rows // 2

    def loads(i):
        chunk = chunk_at(where_ref[i], channels)
        return [
            pltpu.make_async_copy(x_hbm.at[:, :, chunk], x_buf.at[i], load_sem.at[0, i]),
            pltpu.make_async_copy(g_hbm.at[:, chunk], g_buf.at[i], load_sem.at[1, i]),
        ]

    def stores(i):
        chunk = chunk_at(where_ref[i], channels)
        return [
            pltpu.make_async_copy(send_buf.at[i], sends_hbm[i], store_sem.at[0, i]),
            pltpu.make_async_copy(qkv_buf.at[i], qkv_hbm.at[:, :, chunk], store_sem.at[1, i]),
        ]

    for i in range(pieces):
        for copy in loads(i):
            copy.start()
    for i in range(pieces):
        for copy in loads(i):
            copy.wait()

        def body(cols):
            lanes = ext_ref.shape[-1]
            wide = pl.ds(pl.multiple_of(where_ref[i] * channels + cols.start, lanes), lanes)
            for slot in range(2):
                here = slice(slot * half, (slot + 1) * half)
                made = []
                for j in range(3):
                    ext = ext_ref.at[slot * 3 + j]
                    ext[:RIM] = halo_ref[j, :, wide].astype(F32)[slot * RIM : (slot + 1) * RIM]
                    ext[RIM:] = x_buf[i, j, here, cols].astype(F32)
                    total = w_ref[j, :1, wide] * ext[RIM : RIM + half]
                    for s in range(1, tap_count):
                        total = total + w_ref[j, s : s + 1, wide] * ext[RIM - s : RIM - s + half]
                    made.append(total.astype(BF))
                    qkv_buf[i, j, here, cols] = made[j]
                query, key, value = (m.astype(F32) for m in made)
                for a, sent in enumerate((key * value, g_buf[i, here, cols].astype(F32) * query)):
                    turn = ext_ref.at[slot * 3 + a, RIM:]
                    turn[...] = sent
                    for e in range(2):
                        send_buf[i, a, slot, e, :, cols] = turn[pl.ds(e, half // 2, stride=2)].astype(BF)

        each_part(channels, body)
        for copy in stores(i):
            copy.start()
    for i in range(pieces):
        for copy in stores(i):
            copy.wait()


def featurize(chunks, x, g, halo, taps, tap_count):
    rows, width = g.shape
    pieces = chunks.shape[0]
    channels = width // pieces
    *sends, qkv = pl.pallas_call(
        functools.partial(featurize_kernel, tap_count, pieces),
        in_specs=[SCALAR, ANYWHERE, ANYWHERE, VECTOR, VECTOR],
        out_specs=[ANYWHERE] * (pieces + 1),
        out_shape=[jax.ShapeDtypeStruct((2, 2, 2, rows // 4, channels), BF)] * pieces
        + [jax.ShapeDtypeStruct((3, rows, width), BF)],
        scratch_shapes=[
            pltpu.VMEM((pieces, 3, rows, channels), BF),
            pltpu.VMEM((pieces, rows, channels), BF),
            pltpu.VMEM((pieces, 2, 2, 2, rows // 4, channels), BF),
            pltpu.VMEM((pieces, 3, rows, channels), BF),
            pltpu.VMEM((6, rows // 2 + RIM, min(128, channels)), F32),
            pltpu.SemaphoreType.DMA((2, pieces)),
            pltpu.SemaphoreType.DMA((2, pieces)),
        ],
        compiler_params=PARAMS,
    )(chunks, x, g, halo, taps)
    return sends, qkv


def first_row(shape):
    return lax.broadcasted_iota(jnp.int32, shape, 0) == 0


def unite(even, odd, first):
    plus = even[0] + odd[0], even[1] + odd[1]
    minus = even[0] - odd[0], odd[1] - even[1]
    if first is not None:
        plus = plus[0], jnp.where(first, even[1], plus[1])
        minus = minus[0], jnp.where(first, odd[1], minus[1])
    return plus + minus


def divide(spec, first):
    plus_re, plus_im, minus_re, minus_im = spec
    even_im, odd_im = plus_im - minus_im, plus_im + minus_im
    if first is not None:
        even_im, odd_im = jnp.where(first, plus_im, even_im), jnp.where(first, minus_im, odd_im)
    return plus_re + minus_re, even_im, plus_re - minus_re, odd_im


def times(x, f, first, sign):
    def pair(x_re, x_im, f_re, f_im):
        if sign > 0:
            return x_re * f_re - x_im * f_im, x_im * f_re + x_re * f_im
        return x_re * f_re + x_im * f_im, x_im * f_re - x_re * f_im

    out = [*pair(x[0], x[1], f[0], f[1]), *pair(x[2], x[3], f[2], f[3])]
    if first is not None:
        middle_re, middle_im = pair(x[1], x[3], f[1], f[3])
        out = [
            jnp.where(first, 0.5 * (x[0] * f[0]), out[0]),
            jnp.where(first, middle_re, out[1]),
            jnp.where(first, 0.5 * (x[2] * f[2]), out[2]),
            jnp.where(first, middle_im, out[3]),
        ]
    return tuple(out)


def filter_kernel(tile, h_hbm, table_ref, out_hbm, out_buf, turn_ref, seq_ref, load_sem, store_sem):
    segments, _, half, width = out_buf.shape
    lanes = turn_ref.shape[-1]
    size = 2 * half
    steps = half // tile
    parts = [slice(part * lanes, (part + 1) * lanes) for part in range(width // lanes)]
    loads = [pltpu.make_async_copy(h_hbm.at[:, cols], turn_ref.at[i], load_sem.at[i]) for i, cols in enumerate(parts)]

    def store(step):
        at = slice(step * tile, (step + 1) * tile)
        return pltpu.make_async_copy(out_buf.at[:, :, at], out_hbm.at[:, :, at], store_sem.at[step])

    for copy in loads:
        copy.start()
    for i, cols in enumerate(parts):
        loads[i].wait()
        for e in range(2):
            seq_ref[e, :, cols] = turn_ref[i, pl.ds(e, segments * half, stride=2)].astype(BF)
    for step in range(steps):
        at = slice(step * tile, (step + 1) * tile)
        up = slice(half + step * tile, half + (step + 1) * tile)
        first = first_row((tile, width)) if step == 0 else None
        for s in range(segments):
            span = slice(s * half, (s + 1) * half)
            made = [(dot(table_ref[e, at], seq_ref[e, span]), dot(table_ref[e, up], seq_ref[e, span])) for e in range(2)]
            for k, value in enumerate(unite(*made, first)):
                out_buf[s, k, at] = value * (1.0 / size)
        store(step).start()
    for step in range(steps):
        store(step).wait()


def filter_spectrum(h, table):
    size = table.shape[1]
    rows, width = h.shape
    lanes = min(128, width)
    shape = (rows // size, 4, size // 2, width)
    tile = min(128, size // 2)
    return pl.pallas_call(
        functools.partial(filter_kernel, tile),
        in_specs=[ANYWHERE, VECTOR],
        out_specs=ANYWHERE,
        out_shape=jax.ShapeDtypeStruct(shape, F32),
        scratch_shapes=[
            pltpu.VMEM(shape, F32),
            pltpu.VMEM((width // lanes, rows, lanes), F32),
            pltpu.VMEM((2, rows // 2, width), BF),
            pltpu.SemaphoreType.DMA((width // lanes,)),
            pltpu.SemaphoreType.DMA((size // 2 // tile,)),
        ],
        compiler_params=PARAMS,
    )(h, table)


def long_kernel(tile, n, from_ref, to_ref, filt_hbm, table_hbm, back_hbm, *refs):
    recvs_hbm, send_hbm, cross_hbm = refs[:n], refs[n], refs[n + 1]
    filt_ref, table_ref, back_ref, seq_ref, spec_ref, time_ref, cross_ref, mat_ref, const_sem, in_sem, out_sem = refs[n + 2 :]
    _, _, _, quarter, cols = recvs_hbm[0].shape
    _, size, freqs = table_ref.shape
    segments = filt_ref.shape[0]
    constants = [
        pltpu.make_async_copy(source, target, const_sem.at[i])
        for i, (source, target) in enumerate(((table_hbm, table_ref), (filt_hbm, filt_ref), (back_hbm, back_ref)))
    ]

    def block(position):
        return pl.ds(pl.multiple_of(position * quarter, quarter), quarter)

    arrivals = [
        pltpu.make_async_copy(
            recvs_hbm[i].at[:, slot], seq_ref.at[:, :, block(from_ref[2 * i + slot])], in_sem.at[slot, i]
        )
        for i in range(n) for slot in range(2)
    ]

    def departures(a):
        return [
            pltpu.make_async_copy(
                time_ref.at[a, :, block(to_ref[2 * i + slot])], send_hbm.at[i, a, slot], out_sem.at[a, slot, i]
            )
            for i in range(n) for slot in range(2)
        ]

    constants[0].start()
    for copy in arrivals:
        copy.start()
    constants[1].start()
    constants[2].start()
    constants[0].wait()
    for copy in arrivals:
        copy.wait()

    for a in range(2):
        for s in range(segments):
            span = slice(s * freqs, (s + 1) * freqs)
            for e in range(2):
                for step in range(size // tile):
                    at = slice(step * tile, (step + 1) * tile)
                    mat_ref[a, s, e, at] = dot(table_ref[e, at], seq_ref[a, e, span])
    constants[1].wait()

    def total(terms):
        out = terms[0]
        for term in terms[1:]:
            out = tuple(x + y for x, y in zip(out, term))
        return out

    def wrapped(values, p, other, sign):
        if not 0 <= other < segments:
            return values[p]
        return tuple(x + sign * y for x, y in zip(values[p], values[other]))

    def combine(row, lane, first):
        at, up = pl.ds(row, STRIP), pl.ds(freqs + row, STRIP)
        shape = (STRIP, lane.stop - lane.start)
        sign = (1 - 2 * (lax.broadcasted_iota(jnp.int32, shape, 0) % 2)).astype(F32) if segments > 1 else None
        first = first_row(shape) if first else None
        gated, back = (
            [unite(*((mat_ref[a, s, e, at, lane], mat_ref[a, s, e, up, lane]) for e in range(2)), first)
             for s in range(segments)]
            for a in range(2)
        )
        filt = [[filt_ref[s, i, at, lane] for i in range(4)] for s in range(segments)]
        conv = [total([times(gated[p - d], filt[d], first, 1) for d in range(p + 1)]) for p in range(segments)]
        grad = [total([times(back[u], filt[u - p], first, -1) for u in range(p, segments)]) for p in range(segments)]
        cross = [total([times(back[u], gated[u - p], first, -1) for u in range(p, segments)]) for p in range(segments)]
        for p in range(segments):
            for a, value in enumerate((wrapped(conv, p, p - 1, sign), wrapped(grad, p, p + 1, sign))):
                for i, part in enumerate(divide(value, first)):
                    spec_ref[a, i // 2, p, at if i % 2 == 0 else up, lane] = part.astype(BF)
            for i, part in enumerate(divide(wrapped(cross, p, p + 1, sign), first)):
                cross_ref[p, i // 2, at if i % 2 == 0 else up, lane] = part.astype(BF)

    lanes = min(128, cols)
    groups = [slice(part * lanes, (part + 1) * lanes) for part in range(cols // lanes)]

    def strip(i, carry):
        for lane in groups:
            combine(pl.multiple_of(i * STRIP, STRIP), lane, False)
        return carry

    for lane in groups:
        combine(0, lane, True)
    lax.fori_loop(1, freqs // STRIP, strip, 0)
    cross_copy = pltpu.make_async_copy(cross_ref, cross_hbm, const_sem.at[0])
    cross_copy.start()
    constants[2].wait()
    for a in range(2):
        for e in range(2):
            for p in range(segments):
                for step in range(freqs // tile):
                    at = slice(step * tile, (step + 1) * tile)
                    to = slice(p * freqs + step * tile, p * freqs + (step + 1) * tile)
                    time_ref[a, e, to] = dot(back_ref[e, at], spec_ref[a, e, p]).astype(BF)
        for copy in departures(a):
            copy.start()
    for a in range(2):
        for copy in departures(a):
            copy.wait()
    cross_copy.wait()


def long_conv(come_from, go_to, recvs, filt, table, back):
    n = len(recvs)
    _, _, _, quarter, cols = recvs[0].shape
    _, size, freqs = table.shape
    segments = filt.shape[0]
    return pl.pallas_call(
        functools.partial(long_kernel, min(256, freqs), n),
        in_specs=[SCALAR, SCALAR] + [ANYWHERE] * (n + 3),
        out_specs=[ANYWHERE] * 2,
        out_shape=[
            jax.ShapeDtypeStruct((n, 2, 2, 2, quarter, cols), BF),
            jax.ShapeDtypeStruct((segments, 2, size, cols), BF),
        ],
        scratch_shapes=[
            pltpu.VMEM(filt.shape, F32),
            pltpu.VMEM(table.shape, BF),
            pltpu.VMEM(back.shape, BF),
            pltpu.VMEM((2, 2, segments * freqs, cols), BF),
            pltpu.VMEM((2, 2, segments, size, cols), BF),
            pltpu.VMEM((2, 2, segments * freqs, cols), BF),
            pltpu.VMEM((segments, 2, size, cols), BF),
            pltpu.VMEM((2, segments, 2, size, cols), F32),
            pltpu.SemaphoreType.DMA((3,)),
            pltpu.SemaphoreType.DMA((2, n)),
            pltpu.SemaphoreType.DMA((2, 2, n)),
        ],
        compiler_params=PARAMS,
    )(come_from, go_to, filt, table, back, *recvs)


def filter_grad_kernel(cross_ref, back_ref, out_ref, turn_ref):
    segments = cross_ref.shape[0]
    _, freqs, size = back_ref.shape
    parts, _, lanes = turn_ref.shape
    for p in range(segments):
        for e in range(2):
            value = dot(back_ref[e], cross_ref[p, e]) * (1.0 / size)
            for i in range(parts):
                turn_ref[i, pl.ds(p * size + e, freqs, stride=2)] = value[:, i * lanes : (i + 1) * lanes]
    for i in range(parts):
        out_ref[:, i * lanes : (i + 1) * lanes] = turn_ref[i].astype(BF)


def filter_grad(cross, back):
    segments, _, size, cols = cross.shape
    lanes = min(128, cols)
    return pl.pallas_call(
        filter_grad_kernel,
        out_shape=jax.ShapeDtypeStruct((segments * size, cols), BF),
        scratch_shapes=[pltpu.VMEM((cols // lanes, segments * size, lanes), F32)],
        compiler_params=PARAMS,
    )(cross, back)


def in_order(recv, a, slot, cols, turn):
    for e in range(2):
        turn[pl.ds(e, turn.shape[0] // 2, stride=2)] = recv[a, slot, e, :, cols].astype(F32)
    return turn[...]


def tap_kernel(tap_count, recv_hbm, qkv_hbm, x_hbm, g_hbm, halo_ref, short_ref, head_ref,
               recv_buf, kv_buf, x_buf, g_buf, ext_ref, turn_ref, load_sem):
    n, rows, channels = g_buf.shape
    half = rows // 2
    lanes = ext_ref.shape[-1]

    def loads(c):
        chunk = chunk_at(c, channels)
        return [
            pltpu.make_async_copy(recv_hbm.at[c], recv_buf.at[c], load_sem.at[0, c]),
            pltpu.make_async_copy(qkv_hbm.at[1:, :, chunk], kv_buf.at[c], load_sem.at[1, c]),
            pltpu.make_async_copy(x_hbm.at[:, :, chunk], x_buf.at[c], load_sem.at[2, c]),
            pltpu.make_async_copy(g_hbm.at[:, chunk], g_buf.at[c], load_sem.at[3, c]),
        ]

    for c in range(n):
        for copy in loads(c):
            copy.start()

    def one_chunk(c, carry):
        for copy in loads(c):
            copy.wait()

        def body(cols):
            wide = pl.ds(pl.multiple_of(c * channels + cols.start, lanes), lanes)
            short, heads = {}, [[], [], []]
            for slot in range(2):
                here = slice(slot * half, (slot + 1) * half)
                conv, gate = (in_order(recv_buf.at[c], a, slot, cols, turn_ref.at[slot * 2 + a]) for a in range(2))
                key, value = (kv_buf[c, j, here, cols].astype(F32) for j in range(2))
                g = g_buf[c, here, cols].astype(F32)
                grads = ((g * conv).astype(BF).astype(F32), gate * value, gate * key)
                for j in range(3):
                    ext = ext_ref.at[slot * 3 + j]
                    ext[:RIM] = halo_ref[j, :, wide].astype(F32)[slot * RIM : (slot + 1) * RIM]
                    ext[RIM:] = x_buf[c, j, here, cols].astype(F32)
                    heads[j].append(grads[j][:RIM])
                    for s in range(tap_count):
                        term = grads[j] * ext[RIM - s : RIM - s + half]
                        term = jnp.sum(term.reshape(half // 8, 8, lanes), 0)
                        short[s, j] = term if slot == 0 else short[s, j] + term
            lines = []
            for j in range(3):
                lines += [jnp.sum(short[s, j], 0, keepdims=True) for s in range(tap_count)]
                lines.append(jnp.zeros((RIM - tap_count, lanes), F32))
            lines.append(jnp.zeros((short_ref.shape[1] - 3 * RIM, lanes), F32))
            short_ref[c, :, cols] = jnp.concatenate(lines, 0).astype(BF)
            for j in range(3):
                head_ref[j, :, wide] = jnp.concatenate(heads[j], 0).astype(BF)

        each_part(channels, body)
        return carry

    lax.fori_loop(0, n, one_chunk, 0)


def tap_grads(recv, qkv, x, g, halo, tap_count):
    rows, width = g.shape
    n, channels = recv.shape[0], recv.shape[-1]
    lanes = min(128, channels)
    short_rows = -(-3 * RIM // 16) * 16
    return pl.pallas_call(
        functools.partial(tap_kernel, tap_count),
        in_specs=[ANYWHERE] * 4 + [VECTOR],
        out_specs=[VECTOR, VECTOR],
        out_shape=[
            jax.ShapeDtypeStruct((n, short_rows, channels), BF),
            jax.ShapeDtypeStruct((3, 2 * RIM, width), BF),
        ],
        scratch_shapes=[
            pltpu.VMEM(recv.shape, BF),
            pltpu.VMEM((n, 2, rows, channels), BF),
            pltpu.VMEM((n, 3, rows, channels), BF),
            pltpu.VMEM((n, rows, channels), BF),
            pltpu.VMEM((6, rows // 2 + RIM, lanes), F32),
            pltpu.VMEM((4, rows // 2, lanes), F32),
            pltpu.SemaphoreType.DMA((4, n)),
        ],
        compiler_params=PARAMS,
    )(recv, qkv, x, g, halo)


def finish_kernel(tap_count, recv_hbm, qkv_hbm, g_hbm, w_ref, mixed_hbm, grad_hbm, open_ref,
                  recv_buf, qkv_buf, g_buf, mixed_buf, grad_buf, gf_ref, turn_ref, load_sem, store_sem):
    n, rows, channels = g_buf.shape
    half = rows // 2
    lanes = gf_ref.shape[-1]

    def loads(c):
        chunk = chunk_at(c, channels)
        return [
            pltpu.make_async_copy(recv_hbm.at[c], recv_buf.at[c], load_sem.at[0, c]),
            pltpu.make_async_copy(qkv_hbm.at[:, :, chunk], qkv_buf.at[c], load_sem.at[1, c]),
            pltpu.make_async_copy(g_hbm.at[:, chunk], g_buf.at[c], load_sem.at[2, c]),
        ]

    def stores(c):
        chunk = chunk_at(c, channels)
        return [
            pltpu.make_async_copy(mixed_buf.at[c], mixed_hbm.at[:, chunk], store_sem.at[0, c]),
            pltpu.make_async_copy(grad_buf.at[c], grad_hbm.at[:, :, chunk], store_sem.at[1, c]),
        ]

    for c in range(n):
        for copy in loads(c):
            copy.start()

    def one_chunk(c, carry):
        for copy in loads(c):
            copy.wait()

        def body(cols):
            wide = pl.ds(pl.multiple_of(c * channels + cols.start, lanes), lanes)
            rest = [[], [], []]
            for slot in range(2):
                here = slice(slot * half, (slot + 1) * half)
                conv, gate = (in_order(recv_buf.at[c], a, slot, cols, turn_ref.at[slot * 2 + a]) for a in range(2))
                query, key, value = (qkv_buf[c, j, here, cols].astype(F32) for j in range(3))
                g = g_buf[c, here, cols].astype(F32)
                mixed_buf[c, here, cols] = (query * conv).astype(BF)
                grads = ((g * conv).astype(BF).astype(F32), gate * value, gate * key)
                for j in range(3):
                    gf = gf_ref.at[slot * 3 + j]
                    gf[:half] = grads[j]
                    gf[half:] = jnp.zeros((RIM, lanes), F32)
                    total = w_ref[j, :1, wide] * grads[j]
                    for s in range(1, tap_count):
                        total = total + w_ref[j, s : s + 1, wide] * gf[s : s + half]
                    grad_buf[c, j, here, cols] = total.astype(BF)
                    rest[j].append(total[half - RIM :])
            for j in range(3):
                open_ref[j, :, wide] = jnp.concatenate(rest[j], 0)

        each_part(channels, body)
        for copy in stores(c):
            copy.start()
        return carry

    lax.fori_loop(0, n, one_chunk, 0)
    for c in range(n):
        for copy in stores(c):
            copy.wait()


def finish(recv, qkv, g, taps, tap_count):
    rows, width = g.shape
    n, channels = recv.shape[0], recv.shape[-1]
    lanes = min(128, channels)
    return pl.pallas_call(
        functools.partial(finish_kernel, tap_count),
        in_specs=[ANYWHERE] * 3 + [VECTOR],
        out_specs=[ANYWHERE, ANYWHERE, VECTOR],
        out_shape=[
            jax.ShapeDtypeStruct((rows, width), BF),
            jax.ShapeDtypeStruct((3, rows, width), BF),
            jax.ShapeDtypeStruct((3, 2 * RIM, width), F32),
        ],
        scratch_shapes=[
            pltpu.VMEM(recv.shape, BF),
            pltpu.VMEM((n, 3, rows, channels), BF),
            pltpu.VMEM((n, rows, channels), BF),
            pltpu.VMEM((n, rows, channels), BF),
            pltpu.VMEM((n, 3, rows, channels), BF),
            pltpu.VMEM((6, rows // 2 + RIM, lanes), F32),
            pltpu.VMEM((4, rows // 2, lanes), F32),
            pltpu.SemaphoreType.DMA((3, n)),
            pltpu.SemaphoreType.DMA((2, n)),
        ],
        compiler_params=PARAMS,
    )(recv, qkv, g, taps)


def swapped(order_ref):
    me = lax.axis_index("ctx")
    return ((order_ref[2 * me] != me) != (me % 2 == 1)).astype(jnp.int32)


def close_kernel(tap_count, order_ref, old_hbm, open_ref, inner_ref, outer_ref, own_ref, w_ref, grad_hbm,
                 rim_ref, tile_buf, gf_ref, load_sem, store_sem):
    rows = grad_hbm.shape[1]
    tile = 2 * RIM

    def place(slot):
        return grad_hbm.at[:, (slot + 1) * rows // 2 - tile : (slot + 1) * rows // 2]

    def load(slot):
        return pltpu.make_async_copy(place(slot), tile_buf.at[slot], load_sem.at[slot])

    def store(slot):
        return pltpu.make_async_copy(tile_buf.at[slot], place(slot), store_sem.at[slot])

    for slot in range(2):
        load(slot).start()
    swap = swapped(order_ref)
    last = lax.axis_index("ctx") == lax.axis_size("ctx") - 1
    rim_ref[swap] = inner_ref[...].astype(F32)
    rim_ref[1 - swap] = jnp.where(last, own_ref[...].astype(F32), outer_ref[...].astype(F32))
    for slot in range(2):
        load(slot).wait()

    def body(cols):
        for slot in range(2):
            rim = slice(slot * RIM, (slot + 1) * RIM)
            for j in range(3):
                gf = gf_ref.at[slot * 3 + j]
                gf[:RIM] = jnp.zeros((RIM, gf.shape[1]), F32)
                gf[RIM:] = rim_ref[slot, j, :, cols]
                total = open_ref[j, rim, cols]
                for s in range(1, tap_count):
                    total = total + w_ref[j, s : s + 1, cols] * gf[s : s + RIM]
                kept = tile_buf[slot, j, :, cols].astype(F32)[: tile - RIM]
                tile_buf[slot, j, :, cols] = jnp.concatenate([kept, total], 0).astype(BF)

    each_part(grad_hbm.shape[2], body)
    for slot in range(2):
        store(slot).start()
    for slot in range(2):
        store(slot).wait()


def close(order, grads, opened, inner, outer, own, taps, tap_count):
    width = grads.shape[2]
    return pl.pallas_call(
        functools.partial(close_kernel, tap_count),
        in_specs=[SCALAR, ANYWHERE] + [VECTOR] * 5,
        out_specs=ANYWHERE,
        out_shape=jax.ShapeDtypeStruct(grads.shape, BF),
        scratch_shapes=[
            pltpu.VMEM((2, 3, RIM, width), F32),
            pltpu.VMEM((2, 3, 2 * RIM, width), BF),
            pltpu.VMEM((6, 2 * RIM, min(128, width)), F32),
            pltpu.SemaphoreType.DMA((2,)),
            pltpu.SemaphoreType.DMA((2,)),
        ],
        input_output_aliases={1: 0},
        compiler_params=PARAMS,
    )(order, grads, opened, inner, outer, own, taps)


def sum_over_dp(value, keep):
    hop = 1
    total = value
    while hop < lax.axis_size("dp"):
        sent = total.astype(keep)
        other = lax.ppermute(sent, "dp", [(j, j ^ hop) for j in range(lax.axis_size("dp"))])
        total = sent.astype(F32) + other.astype(F32)
        hop *= 2
    return total


def on_device(feats, grad_y, short_w, long_h, block_order):
    n = lax.axis_size("ctx")
    me = lax.axis_index("ctx")
    _, _, rows, width = feats.shape
    half = rows // 2
    channels = width // n
    tap_count = short_w.shape[0]
    table, back = (jnp.asarray(t) for t in dft_tables(min(rows * n, 1024)))
    taps = short_w.transpose(1, 0, 2)
    x, g = feats[0], grad_y[0]
    numbers = jnp.arange(2 * n, dtype=jnp.int32)
    flip = jnp.sum(jnp.where(numbers == 2 * me, block_order, 0)) != me
    swap = flip != (me % 2 == 1)
    last = me == n - 1

    def trade(inner, outer):
        got_inner = lax.ppermute(inner, "ctx", [(j, j ^ 1) for j in range(n)])
        got_outer = lax.ppermute(outer, "ctx", [(j, j + 1 if j % 2 else j - 1) for j in range(1, n - 1)])
        return got_inner, got_outer

    tails = x[:, half - RIM : half], x[:, rows - RIM :]
    own = jnp.where(swap, tails[0], tails[1])
    inner, outer = trade(jnp.where(swap, tails[1], tails[0]), own)
    outer = jnp.where(last, own, outer)
    halo = jnp.concatenate([jnp.where(swap, inner, outer), jnp.where(swap, outer, inner)], 1)
    hops = sorted(range(1, n), key=lambda s: (s != 2, abs(s - n // 2))) + [0]
    chunks = (me + jnp.asarray(hops, jnp.int32)) % n
    sends, qkv = featurize(chunks, x, g, halo, taps, tap_count)
    recvs = [lax.ppermute(sent, "ctx", [(j, (j + s) % n) for j in range(n)]) if s else sent
             for s, sent in zip(hops, sends)]
    long_h, qkv = lax.optimization_barrier((long_h, qkv))
    filt = filter_spectrum(long_h, table)
    origins = (me - jnp.asarray(hops, jnp.int32) + n) % n
    wanted = 2 * jnp.repeat(origins, 2) + numbers % 2
    come_from = jnp.sum(jnp.where(wanted[:, None] == numbers[None, :], block_order[None, :], 0), 1).astype(jnp.int32)
    out, cross = long_conv(come_from, block_order, recvs, filt, table, back)

    returned = lax.all_to_all(out, "ctx", 0, 0, tiled=True)
    filter_sum = sum_over_dp(filter_grad(cross, back), BF)
    returned, filter_sum = lax.optimization_barrier((returned, filter_sum))
    short, heads = tap_grads(returned, qkv, x, g, halo, tap_count)
    pieces = lax.all_to_all(short, "ctx", 0, 0, tiled=True)
    heads = heads[:, :RIM], heads[:, RIM:]
    own = jnp.where(swap, heads[1], heads[0])
    inner, outer = trade(jnp.where(swap, heads[0], heads[1]), own)
    mixed, grads, opened = finish(returned, qkv, g, taps, tap_count)
    pieces, inner, outer, opened = lax.optimization_barrier((pieces, inner, outer, opened))
    grads = close(block_order, grads, opened, inner, outer, own, taps, tap_count)
    short_sum = sum_over_dp(jnp.sum(pieces.astype(F32), 0)[: 3 * RIM], F32)
    short_sum = short_sum.reshape(3, RIM, channels)[:, :tap_count].transpose(1, 0, 2)
    return mixed[None], grads[None], short_sum, filter_sum


def solution(mesh):
    placed = (P("dp", None, "ctx", None), P("dp", "ctx", None), P(), P(None, "ctx"), P())
    return jax.shard_map(
        on_device,
        mesh=mesh,
        in_specs=placed,
        out_specs=(
            P("dp", "ctx", None),
            P("dp", None, "ctx", None),
            P(None, None, "ctx"),
            P(None, "ctx"),
        ),
        check_vma=False,
    )
```
